256 devices in a mesh: clus: 16 (over z, core), node: 16 (over x, y).
Axes of the slice: x: 4, y: 4, z: 8, core: 2. Of those that a mesh axis runs over, the one named last changes fastest.
Arguments:
- node_feats: bfloat16 [16, 2048, 1024], P('clus', 'node'), may hold values from -6 to 6
- cotangent: bfloat16 [16, 2048, 1024], P('clus', 'node'), may hold values from -6 to 6
- w_query: bfloat16 [1024, 1024], replicated, may hold values from -0.1875 to 0.1875
- w_key: bfloat16 [1024, 1024], replicated, may hold values from -0.1875 to 0.1875
- w_value: bfloat16 [1024, 1024], replicated, may hold values from -0.1875 to 0.1875
- w_out: bfloat16 [1024, 1024], replicated, may hold values from -0.1875 to 0.1875
- eigvec: bfloat16 [16, 64, 2048], P('clus'), may hold values from -3.5 to 3.5
- eig_weight: float32 [16, 64], P('node'), may hold values from 0.1 to 1
- block_mask: int32 [16, 16, 16, 16], P('clus', 'node'), may hold values from 0 to 1, as said below
Outputs:
- grad_nodes: bfloat16 [16, 2048, 1024], P('clus', 'node')
- grad_eigvec: float32 [16, 64, 2048], P('clus', None, 'node')
- grad_weight: float32 [16, 64], P('node')
- grad_proj: float32 [4, 1024, 1024], P(None, 'clus', 'node')
The draws below stay inside these ranges and needn't reach their ends.
Inputs may be any that keep to these rules, and one draw needn't show every extreme that they name: `block_mask`: each entry is 0 or 1; every diagonal tile is 1; the share of present tiles differs between clusters and heads.
All inputs are finite; a program needn't handle non-finite values.
Results may differ from the reference program's by a relative error of at most 0.012.
The reference program's roundings to bfloat16 on the way (of `weighted`, `prob_half`, `output` and `dscore`) count: a program that leaves them out, or rounds other values in their place, can miss the bound.
Values may be sent and summed in bfloat16 or wider, within the bound.
A program may use at most 128 MiB of HBM per device.

```python
import math
import jax
import jax.numpy as jnp
from jax import lax

H = 16
EIG = 64
TILE = 128
D = 1024
NC = 2048
NB = 16
CLUSTERS = 16


def draw_eigvec(key, part):
    sub_keys = jax.random.split(key, 2)
    values = jnp.clip(0.3 * jax.random.normal(sub_keys[1], (CLUSTERS, EIG, NC), jnp.float32), -3.5, 3.5)
    return values.astype(jnp.bfloat16)


def draw_block_mask(key, part):
    sub_keys = jax.random.split(key, 2)
    levels = jax.random.randint(sub_keys[0], (CLUSTERS, H, 1, 1), 2, 7)
    chosen = jax.random.randint(sub_keys[1], (CLUSTERS, H, NB, NB), 0, 8) < levels
    diagonal = jnp.arange(NB)[:, None] == jnp.arange(NB)[None, :]
    return jnp.where(chosen | diagonal[None, None], 1, 0).astype(jnp.int32)


def spiked(array, own_key, source, target, parts, factor):
    owner, partner = [(jnp.arange(array.shape[axis_at]) // (array.shape[axis_at] // parts)).reshape([-1 if axis == axis_at else 1 for axis in range(array.ndim)]) for axis_at in (source, target)]
    chosen = jax.random.permutation(own_key, parts)[partner]
    strong = (owner == chosen) | (owner == (partner + parts // 2) % parts)
    return jnp.where(strong, factor * array, array)


def shard_levels(rng, shape, shards, low, largest):
    gain = 1.0
    for position, blocks in shards:
        steps = jax.random.uniform(jax.random.fold_in(jax.random.fold_in(rng, 6), position), (blocks,), jnp.float32, low / len(shards), largest / len(shards))
        gain = gain * jnp.repeat(jnp.exp(steps), shape[position] // blocks).reshape((-1,) + (1,) * (len(shape) - 1 - position))
    return gain


def normal_values(rng, shape, scale, reach, cuts=(), held_as=jnp.bfloat16):
    level = shard_levels(rng, shape, cuts, -0.22, 0.18) if cuts else 1.0
    values = jax.random.normal(rng, shape, jnp.float32) * scale * level
    return jnp.minimum(jnp.maximum(values, -reach), reach).astype(held_as)


def noise_with(rng, extent, scale, bound, shards, heavy, held_as=jnp.bfloat16):
    drawn = scale * jax.random.normal(rng, extent, jnp.float32)
    if shards:
        drawn = drawn * shard_levels(rng, extent, shards, -0.22, 0.18)
    return jnp.clip(spiked(drawn, jax.random.fold_in(rng, 3), *heavy), -bound, bound).astype(held_as)


def setup_inputs(seed: int = 0) -> dict:
    splits = jax.random.split(jax.random.key(seed), 10)
    return {
        "node_feats": noise_with(splits[0], (CLUSTERS, NC, D), 1.0, 6.0, ((0, 16), (1, 16)), (1, 2, 16, 2.0)),
        "cotangent": normal_values(splits[1], (CLUSTERS, NC, D), 1.0, 6.0, ((0, 16), (1, 16))),
        "w_query": normal_values(splits[2], (D, D), D ** -0.5, 0.1875),
        "w_key": normal_values(splits[3], (D, D), D ** -0.5, 0.1875),
        "w_value": normal_values(splits[4], (D, D), D ** -0.5, 0.1875),
        "w_out": normal_values(splits[5], (D, D), D ** -0.5, 0.1875),
        "eigvec": draw_eigvec(jax.random.fold_in(splits[9], 71), 0),
        "eig_weight": jnp.clip(jnp.exp(math.log(1.0) - 2.3025851 * jax.random.uniform(splits[7], (H, EIG), jnp.float32) ** shard_levels(splits[7], (H, EIG), ((0, 16),), -0.2, 0.2)), 0.1, 1.0),
        "block_mask": draw_block_mask(jax.random.fold_in(splits[9], 71), 0),
    }


def attend_head(eigvec_c, query, keys_all, values_all, dout_head, lam_head, mask_head):
    score_scale = query.shape[1] ** -0.5
    eig_float = eigvec_c.astype(jnp.float32)
    weighted = (lam_head[:, None] * eig_float).astype(jnp.bfloat16)
    eig_bias = jnp.dot(eigvec_c.T, weighted, preferred_element_type=jnp.float32)
    scores = jnp.dot(query, keys_all.T, preferred_element_type=jnp.float32) * score_scale + eig_bias
    present = jnp.repeat(jnp.repeat(mask_head, TILE, axis=0), TILE, axis=1) > 0
    masked = jnp.where(present, scores, -jnp.inf)
    row_max = jnp.max(masked, axis=1, keepdims=True)
    raised = jnp.exp(masked - row_max)
    attn_prob = raised / jnp.sum(raised, axis=1, keepdims=True)
    prob_half = attn_prob.astype(jnp.bfloat16)
    output = jnp.dot(prob_half, values_all, preferred_element_type=jnp.float32).astype(jnp.bfloat16)
    dprob = jnp.dot(dout_head, values_all.T, preferred_element_type=jnp.float32)
    row_delta = jnp.sum(attn_prob * dprob, axis=1, keepdims=True)
    dscore = (attn_prob * (dprob - row_delta)).astype(jnp.bfloat16)
    query_grad = (jnp.dot(dscore, keys_all, preferred_element_type=jnp.float32) * score_scale).astype(jnp.bfloat16)
    key_grad = (jnp.dot(dscore.T, query, preferred_element_type=jnp.float32) * score_scale).astype(jnp.bfloat16)
    value_grad = jnp.dot(prob_half.T, dout_head, preferred_element_type=jnp.float32).astype(jnp.bfloat16)
    eig_left = jnp.dot(dscore, eigvec_c.T, preferred_element_type=jnp.float32)
    eig_right = jnp.dot(dscore.T, eigvec_c.T, preferred_element_type=jnp.float32)
    weight_grad = jnp.sum(eig_float.T * eig_left, axis=0)
    eig_grad = lam_head[None, :] * (eig_left + eig_right)
    return output, query_grad, key_grad, value_grad, weight_grad, eig_grad


def reference(node_feats, cotangent, w_query, w_key, w_value, w_out, eigvec, eig_weight, block_mask):
    node_count = node_feats.shape[1]
    model_width = node_feats.shape[2]
    head_count = eig_weight.shape[0]
    head_size = model_width // head_count

    def by_head(matrix):
        return matrix.reshape(node_count, head_count, head_size).transpose(1, 0, 2)

    def merged(stacked):
        return stacked.transpose(1, 0, 2).reshape(node_count, model_width)

    def one_cluster(totals, inputs):
        node_rows, grads_in, eigvec_c, mask_c = inputs
        query = jnp.dot(node_rows, w_query, preferred_element_type=jnp.float32).astype(jnp.bfloat16)
        keys_all = jnp.dot(node_rows, w_key, preferred_element_type=jnp.float32).astype(jnp.bfloat16)
        values_all = jnp.dot(node_rows, w_value, preferred_element_type=jnp.float32).astype(jnp.bfloat16)
        d_att = jnp.dot(grads_in, w_out, preferred_element_type=jnp.float32).astype(jnp.bfloat16)

        def one_head(items):
            return attend_head(eigvec_c, items[0], items[1], items[2], items[3], items[4], items[5])

        results = lax.map(one_head, (by_head(query), by_head(keys_all), by_head(values_all), by_head(d_att), eig_weight, mask_c))
        output = merged(results[0])
        query_grad = merged(results[1])
        key_grad = merged(results[2])
        value_grad = merged(results[3])
        grad_rows = (jnp.dot(query_grad, w_query.T, preferred_element_type=jnp.float32)
                     + jnp.dot(key_grad, w_key.T, preferred_element_type=jnp.float32)
                     + jnp.dot(value_grad, w_value.T, preferred_element_type=jnp.float32)).astype(jnp.bfloat16)
        grad_terms = jnp.stack([
            jnp.dot(node_rows.T, query_grad, preferred_element_type=jnp.float32),
            jnp.dot(node_rows.T, key_grad, preferred_element_type=jnp.float32),
            jnp.dot(node_rows.T, value_grad, preferred_element_type=jnp.float32),
            jnp.dot(grads_in.T, output, preferred_element_type=jnp.float32)])
        new_totals = (totals[0] + grad_terms, totals[1] + results[4])
        return new_totals, (grad_rows, jnp.sum(results[5], axis=0).T)

    initial = (jnp.zeros((4, model_width, model_width), jnp.float32), jnp.zeros(eig_weight.shape, jnp.float32))
    totals, stacked = lax.scan(one_cluster, initial, (node_feats, cotangent, eigvec, block_mask))
    return stacked[0], stacked[1], totals[1], totals[0]
```

```python
import functools

import jax
import jax.numpy as jnp
from jax import lax
from jax.experimental import pallas as pl
from jax.experimental.pallas import tpu as pltpu
from jax.sharding import PartitionSpec as P

MESH = pl.DeviceIdType.MESH
F32 = jnp.float32
BF16 = jnp.bfloat16
ABSENT = -(2.0**100)
SIDE = 4
NODES = 16
TOK = 128
D = 1024
NC = 2048
EIG = 64
HS = 64
SCALE = HS**-0.5
ROWS = 256


def dot(a, b):
    return lax.dot_general(a, b, (((1,), (0,)), ((), ())), preferred_element_type=F32)


def kernel(
    clusters,
    x_hbm, cot_hbm, wq_hbm, wk_hbm, wv_hbm, wo_hbm, eig_ref, lam_ref, mask_ref,
    gn_ref, ge_ref, gw_ref, gp_ref,
    w, xg, cg, send, recv, eigt, qe, d0, ke, bm, eqt, dt, kt, bt,
    acc_k, acc_v, grads, left, back, gs, gr,
    in_sem, w_sem, ring_send, ring_recv, f_send, f_recv, b_send, b_recv, c_send, c_recv,
):
    n = lax.axis_index("node")
    c = lax.axis_index("clus")
    mx = lax.div(n, SIDE)
    my = lax.rem(n, SIDE)
    chunk = D // clusters

    def turn(i, by):
        return lax.rem(i + by, SIDE)

    x_in = pltpu.make_async_copy(x_hbm, xg.at[mx, my], in_sem.at[0])
    c_in = pltpu.make_async_copy(cot_hbm, cg.at[mx, my], in_sem.at[1])
    x_in.start()
    c_in.start()
    w_hbm = (wq_hbm, wk_hbm, wv_hbm, wo_hbm)

    def w_copy(t, k):
        cols = pl.ds(pl.multiple_of(turn(mx, k) * 256, 256), 256)
        return pltpu.make_async_copy(w_hbm[t].at[:, cols], w.at[t, :, cols], w_sem.at[t, k])

    for k in range(SIDE):
        for t in range(4):
            w_copy(t, k).start()

    barrier = pltpu.get_barrier_semaphore()

    @pl.loop(1, NODES)
    def _(k):
        pl.semaphore_signal(barrier, inc=1, device_id={"node": lax.rem(n + k, NODES)}, device_id_type=MESH)

    if clusters > 1:
        @pl.loop(1, clusters)
        def _(k):
            pl.semaphore_signal(
                barrier, inc=1, device_id={"clus": lax.rem(c + k, clusters)}, device_id_type=MESH
            )

    row_id = lax.broadcasted_iota(jnp.int32, (EIG, EIG), 0)
    col_id = lax.broadcasted_iota(jnp.int32, (EIG, EIG), 1)
    lam = jnp.sum(jnp.where(row_id == col_id, lam_ref[...], 0.0), axis=1, keepdims=True)
    kt[64:128, :] = (lam * eig_ref[...].astype(F32)).astype(BF16)
    kt[144:256, :] = jnp.zeros((112, NC), BF16)
    bias = jnp.where(mask_ref[...] > 0, 0.0, ABSENT)
    for j in range(NODES):
        kt[128:144, j * TOK : (j + 1) * TOK] = jnp.broadcast_to(bias[:, j : j + 1], (16, TOK)).astype(BF16)
        part = eig_ref[:, j * TOK : (j + 1) * TOK].astype(F32)
        full = jnp.concatenate([jnp.zeros((64, TOK), F32), part], axis=0)
        eigt[j * TOK : (j + 1) * TOK, :] = full.T.astype(BF16)
    eqt[64:128, :] = eig_ref[...]

    x_in.wait()
    c_in.wait()
    pl.semaphore_wait(barrier, NODES - 1 + clusters - 1)

    def copy_to(src, dst, send_sem, recv_sem, node):
        return pltpu.make_async_remote_copy(
            src_ref=src, dst_ref=dst, send_sem=send_sem, recv_sem=recv_sem,
            device_id={"node": node}, device_id_type=MESH,
        )

    def x_line(i, lo, size):
        return xg.at[mx, i, pl.ds(lo, size)]

    def c_line(i, lo, size):
        return cg.at[i, my, pl.ds(lo, size)]

    def x_group(i, half):
        return xg.at[i, pl.ds(2 * half, 2)]

    def c_group(i, half):
        return cg.at[pl.ds(2 * half, 2), i]

    def x_along(by):
        return mx * SIDE + turn(my, by)

    def c_along(by):
        return turn(mx, by) * SIDE + my

    rings = []
    for which, line, group, one, two, p1, p2 in (
        (0, x_line, x_group, x_along, c_along, my, mx),
        (1, c_line, c_group, c_along, x_along, mx, my),
    ):
        rings.append((
            [(0, line(p1, 0, TOK), line(turn(p1, 3), 0, TOK), one(1)),
             (1, line(p1, 0, TOK), line(turn(p1, 1), 0, TOK), one(3))],
            [(2, line(turn(p1, 3), 0, 64), line(turn(p1, 2), 0, 64), one(1)),
             (3, line(turn(p1, 1), 64, 64), line(turn(p1, 2), 64, 64), one(3))],
            [(4, group(p2, 0), group(turn(p2, 3), 0), two(1)),
             (5, group(p2, 1), group(turn(p2, 1), 1), two(3))],
            [(6, group(p2, 1), group(turn(p2, 3), 1), two(1)),
             (7, group(p2, 0), group(turn(p2, 1), 0), two(3))],
            [(8, group(turn(p2, 3), 0), group(turn(p2, 2), 0), two(1)),
             (9, group(turn(p2, 1), 1), group(turn(p2, 2), 1), two(3))],
        ))

    def ring(stage, action):
        for which in range(2):
            for number, out, into, node in rings[which][stage]:
                sems = ring_send.at[which, number], ring_recv.at[which, number]
                if action == "start":
                    copy_to(out, out, *sems, node).start()
                elif action == "recv":
                    copy_to(into, into, *sems, node).wait_recv()
                else:
                    copy_to(out, out, *sems, node).wait_send()

    ring(0, "start")

    low = lax.broadcasted_iota(jnp.int32, (TOK, 128), 1) < 64

    def forward(t):
        return copy_to(send.at[t], recv.at[n], f_send.at[t], f_recv.at[n], t)

    def forward_self():
        return pltpu.make_async_copy(send.at[n], recv.at[n], f_recv.at[n])

    for k in range(SIDE):
        first = turn(mx, k) * SIDE
        cols = pl.ds(pl.multiple_of(first * HS, 256), 256)
        rows_x = xg[mx, my]
        parts = []
        for t in range(4):
            w_copy(t, k).wait()
            rows_in = rows_x if t < 3 else cg[mx, my]
            part = dot(rows_in, w[t, :, cols])
            parts.append(part * SCALE if t == 0 else part)
        for pair in range(2):
            q, kk, v, d = (part[:, pair * 128 : (pair + 1) * 128] for part in parts)
            qs, ks, vs, ds = (pltpu.roll(a, 64, 1) for a in (q, kk, v, d))
            t0 = first + 2 * pair
            send[t0, :, 0:128] = jnp.where(low, q, ds).astype(BF16)
            send[t0, :, 128:256] = jnp.where(low, kk, vs).astype(BF16)
            send[t0 + 1, :, 0:128] = jnp.where(low, qs, d).astype(BF16)
            send[t0 + 1, :, 128:256] = jnp.where(low, ks, v).astype(BF16)
        for j in range(SIDE):
            t = first + j

            @pl.when(t != n)
            def _():
                forward(t).start()

            @pl.when(t == n)
            def _():
                forward_self().start()

    ring(0, "recv")
    ring(1, "start")

    acc_k[...] = jnp.zeros_like(acc_k)
    acc_v[...] = jnp.zeros_like(acc_v)

    @pl.loop(0, NODES)
    def _(k):
        s = lax.rem(n + k, NODES)

        @pl.when(s != n)
        def _():
            copy_to(recv.at[s], recv.at[s], f_send.at[s], f_recv.at[s], s).wait_recv()

        @pl.when(s == n)
        def _():
            forward_self().wait()

        rows = pl.ds(pl.multiple_of(s * TOK, TOK), TOK)
        a = recv[s, :, 0:128].astype(F32)
        b = recv[s, :, 128:256].astype(F32)
        e = eigt[rows, :].astype(F32)
        qe[rows, :] = jnp.where(low, a, e).astype(BF16)
        ke[rows, :] = jnp.where(low, b, e).astype(BF16)
        d0[rows, :] = jnp.where(low, 0.0, a).astype(BF16)
        bm[rows, :] = b.astype(BF16)
        at = a.T.astype(BF16)
        b_t = b.T.astype(BF16)
        eqt[0:64, rows] = at[0:64]
        dt[:, rows] = at[64:128]
        kt[0:64, rows] = b_t[0:64]
        bt[:, rows] = b_t

    ring(1, "recv")
    ring(2, "start")
    ring(3, "start")

    lane = lax.broadcasted_iota(jnp.int32, (ROWS, 128), 1)
    sub = lax.div(lax.broadcasted_iota(jnp.int32, (ROWS, 128), 0), TOK)
    steps = NC // ROWS

    @pl.loop(0, steps)
    def _(i):
        @pl.when(i == steps // 2)
        def _():
            ring(2, "recv")
            ring(4, "start")

        rows = pl.ds(pl.multiple_of(i * ROWS, ROWS), ROWS)
        tile = jnp.where(lane == sub + i * (ROWS // TOK), 1.0, 0.0).astype(BF16)
        scores = dot(jnp.concatenate([qe[rows, :], tile], axis=1), kt[...])
        dprob = dot(d0[rows, :], bt[...])
        raised = jnp.exp(scores - jnp.max(scores, axis=1, keepdims=True))
        inverse = 1.0 / jnp.sum(raised, axis=1, keepdims=True)
        prob = raised * inverse
        delta = jnp.sum(prob * dprob, axis=1, keepdims=True)
        half = prob.astype(BF16)
        dscore = (prob * (dprob - delta)).astype(BF16)
        out = dot(half, bm[...])
        grad_q = dot(dscore, ke[...])
        acc_k[...] += dot(eqt[:, rows], dscore)
        acc_v[...] += dot(dt[:, rows], half)
        grad_qt = grad_q.T
        grads[0, :, rows] = (grad_qt[0:64] * SCALE).astype(BF16)
        left[:, rows] = grad_qt[64:128]
        grads[4, :, rows] = out.T[64:128].astype(BF16)

    grads[1] = acc_k[0:64].astype(BF16)
    grads[2] = acc_v[...].astype(BF16)
    left_all = left[...]
    grads[3] = (lam * (left_all + acc_k[64:128])).astype(BF16)

    def backward(t):
        return copy_to(
            grads.at[pl.ds(0, 4), :, pl.ds(pl.multiple_of(t * TOK, TOK), TOK)],
            back.at[:, pl.ds(pl.multiple_of(n * HS, HS), HS), :],
            b_send.at[t], b_recv.at[n], t,
        )

    def landed(s):
        return back.at[:, pl.ds(pl.multiple_of(s * HS, HS), HS), :]

    def backward_self():
        return pltpu.make_async_copy(
            grads.at[pl.ds(0, 4), :, pl.ds(pl.multiple_of(n * TOK, TOK), TOK)], landed(n), b_recv.at[n]
        )

    backward_self().start()

    @pl.loop(1, NODES)
    def _(k):
        backward(lax.rem(n + k, NODES)).start()

    weight_col = jnp.sum(eig_ref[...].astype(F32) * left_all, axis=1, keepdims=True)
    row_w = lax.broadcasted_iota(jnp.int32, (EIG, 256), 0)
    col_w = lax.broadcasted_iota(jnp.int32, (EIG, 256), 1)
    weight_row = jnp.sum(jnp.where(row_w == col_w, weight_col, 0.0), axis=0, keepdims=True)
    weight_high = weight_row.astype(BF16).astype(F32)
    row_g = lax.broadcasted_iota(jnp.int32, (16, 256), 0)
    weight_part = jnp.where(
        row_g == 0, weight_high, jnp.where(row_g == 1, weight_row - weight_high, 0.0)
    ).astype(BF16)

    ring(3, "recv")
    ring(4, "recv")

    def across(t):
        return pltpu.make_async_remote_copy(
            src_ref=gs.at[t], dst_ref=gr.at[c], send_sem=c_send.at[t], recv_sem=c_recv.at[c],
            device_id={"clus": t}, device_id_type=MESH,
        )

    def across_in(s):
        return pltpu.make_async_remote_copy(
            src_ref=gr.at[s], dst_ref=gr.at[s], send_sem=c_send.at[s], recv_sem=c_recv.at[s],
            device_id={"clus": s}, device_id_type=MESH,
        )

    def across_self():
        return pltpu.make_async_copy(gs.at[c], gr.at[c], c_recv.at[c])

    for m in range(4):
        cols = slice(m * 256, (m + 1) * 256)
        gx = dot(grads[0:3].reshape(192, NC), xg[:, :, :, cols].reshape(NC, 256))
        gc = dot(grads[4], cg[:, :, :, cols].reshape(NC, 256))
        g = jnp.concatenate([gx, gc], axis=0).T.astype(BF16)
        size = min(chunk, 256)
        for part in range(256 // size):
            owner, lo = divmod(m * 256 + part * size, chunk)
            gs[owner, lo : lo + size, :] = g[part * size : (part + 1) * size]
            if lo + size == chunk:
                gs[owner, chunk : chunk + 16, :] = weight_part

                @pl.when(c != owner)
                def _():
                    across(owner).start()

                @pl.when(c == owner)
                def _():
                    across_self().start()

    backward_self().wait()

    @pl.loop(1, NODES)
    def _(k):
        s = lax.rem(n + k, NODES)
        copy_to(landed(s), landed(s), b_send.at[s], b_recv.at[s], s).wait_recv()

    for m in range(4):
        rows = slice(m * 256, (m + 1) * 256)
        total = dot(w[0, rows, :], back[0]) + dot(w[1, rows, :], back[1]) + dot(w[2, rows, :], back[2])
        gn_ref[:, rows] = total.T.astype(BF16)
    eig_total = back[3, 0:64, :].astype(F32)
    for s in range(1, NODES):
        eig_total += back[3, s * 64 : (s + 1) * 64, :].astype(F32)
    ge_ref[...] = eig_total

    across_self().wait()
    if clusters > 1:
        @pl.loop(1, clusters)
        def _(k):
            across_in(lax.rem(c + k, clusters)).wait_recv()

    total = gr[0].astype(F32)
    for s in range(1, clusters):
        total += gr[s].astype(F32)
    for pair in range(2):
        both = total[0:chunk, pair * 128 : (pair + 1) * 128]
        gp_ref[2 * pair] = both[:, 0:64]
        gp_ref[2 * pair + 1] = pltpu.roll(both, 64, 1)[:, 0:64]
    gw_ref[...] = (total[chunk : chunk + 1] + total[chunk + 1 : chunk + 2])[:, 0:64]

    for stage in range(5):
        ring(stage, "send")

    @pl.loop(1, NODES)
    def _(k):
        t = lax.rem(n + k, NODES)
        forward(t).wait_send()
        backward(t).wait_send()

    if clusters > 1:
        @pl.loop(1, clusters)
        def _(k):
            across(lax.rem(c + k, clusters)).wait_send()


def body(clusters, node_feats, cotangent, w_query, w_key, w_value, w_out, eigvec, eig_weight, block_mask):
    chunk = D // clusters
    anywhere = pl.BlockSpec(memory_space=pl.ANY)
    vmem = pl.BlockSpec(memory_space=pltpu.VMEM)
    dma = pltpu.SemaphoreType.DMA
    gn, ge, gw, gp = pl.pallas_call(
        functools.partial(kernel, clusters),
        out_shape=(
            jax.ShapeDtypeStruct((TOK, D), BF16),
            jax.ShapeDtypeStruct((EIG, TOK), F32),
            jax.ShapeDtypeStruct((1, EIG), F32),
            jax.ShapeDtypeStruct((4, chunk, HS), F32),
        ),
        in_specs=[anywhere] * 6 + [vmem] * 3,
        out_specs=(vmem,) * 4,
        scratch_shapes=[
            pltpu.VMEM((4, D, D), BF16),
            pltpu.VMEM((SIDE, SIDE, TOK, D), BF16),
            pltpu.VMEM((SIDE, SIDE, TOK, D), BF16),
            pltpu.VMEM((NODES, TOK, 256), BF16),
            pltpu.VMEM((NODES, TOK, 256), BF16),
            pltpu.VMEM((NC, 128), BF16),
            pltpu.VMEM((NC, 128), BF16),
            pltpu.VMEM((NC, 128), BF16),
            pltpu.VMEM((NC, 128), BF16),
            pltpu.VMEM((NC, 128), BF16),
            pltpu.VMEM((128, NC), BF16),
            pltpu.VMEM((64, NC), BF16),
            pltpu.VMEM((256, NC), BF16),
            pltpu.VMEM((128, NC), BF16),
            pltpu.VMEM((128, NC), F32),
            pltpu.VMEM((64, NC), F32),
            pltpu.VMEM((5, 64, NC), BF16),
            pltpu.VMEM((64, NC), F32),
            pltpu.VMEM((4, D, TOK), BF16),
            pltpu.VMEM((clusters, chunk + 16, 256), BF16),
            pltpu.VMEM((clusters, chunk + 16, 256), BF16),
            dma((2,)),
            dma((4, 4)),
            dma((2, 10)),
            dma((2, 10)),
            dma((NODES,)),
            dma((NODES,)),
            dma((NODES,)),
            dma((NODES,)),
            dma((clusters,)),
            dma((clusters,)),
        ],
        compiler_params=pltpu.CompilerParams(
            collective_id=0, has_side_effects=True, vmem_limit_bytes=60 * 1024 * 1024
        ),
        cost_estimate=pl.CostEstimate(flops=8 * 10**9, bytes_accessed=10**7, transcendentals=4 * 10**6),
    )(
        node_feats[0], cotangent[0], w_query, w_key, w_value, w_out,
        eigvec[0], eig_weight, block_mask[0, 0],
    )
    return gn[None], ge[None], gw, gp


def solution(mesh):
    placed = (
        P("clus", "node", None),
        P("clus", "node", None),
        P(),
        P(),
        P(),
        P(),
        P("clus", None, None),
        P("node", None),
        P("clus", "node", None, None),
    )
    return jax.shard_map(
        functools.partial(body, mesh.shape["clus"]),
        mesh=mesh,
        in_specs=placed,
        out_specs=(
            P("clus", "node", None),
            P("clus", None, "node"),
            P("node", None),
            P(None, "clus", "node"),
        ),
        check_vma=False,
    )
```

```python
import functools

import jax
import jax.numpy as jnp
from jax import lax
from jax.experimental import pallas as pl
from jax.experimental.pallas import tpu as pltpu
from jax.sharding import PartitionSpec as P

MESH = pl.DeviceIdType.MESH
F32 = jnp.float32
BF16 = jnp.bfloat16
ABSENT = -(2.0**100)
SIDE = 4
NODES = 16
TOK = 128
D = 1024
NC = 2048
EIG = 64
HS = 64
SCALE = HS**-0.5
ROWS = 256


def dot(a, b):
    return lax.dot_general(a, b, (((1,), (0,)), ((), ())), preferred_element_type=F32)


def kernel(
    clusters,
    x_hbm, cot_hbm, wq_hbm, wk_hbm, wv_hbm, wo_hbm, eig_ref, lam_ref, mask_ref,
    gn_ref, ge_ref, gw_ref, gp_ref,
    w, xlx, xly, cly, send, recv, eigt, qe, d0, ke, bm, eqt, dt, kt, bt,
    acc_k, acc_v, grads, left, back, ha, hb, part, sums, gs, gr,
    in_sem, w_sem, ring_send, ring_recv, f_send, f_recv, b_send, b_recv, e_send, e_recv, l_send, l_recv,
    p_send, p_recv, c_send, c_recv,
):
    n = lax.axis_index("node")
    c = lax.axis_index("clus")
    mx = lax.div(n, SIDE)
    my = lax.rem(n, SIDE)
    chunk = D // clusters

    def turn(i, by):
        return lax.rem(i + by, SIDE)

    loads = [
        pltpu.make_async_copy(x_hbm, xlx.at[mx], in_sem.at[0]),
        pltpu.make_async_copy(x_hbm, xly.at[my], in_sem.at[1]),
        pltpu.make_async_copy(cot_hbm, cly.at[my], in_sem.at[2]),
    ]
    for load in loads:
        load.start()
    w_hbm = (wq_hbm, wk_hbm, wv_hbm, wo_hbm)

    def w_copy(t, k):
        cols = pl.ds(pl.multiple_of(turn(mx, k) * 256, 256), 256)
        return pltpu.make_async_copy(w_hbm[t].at[:, cols], w.at[t, :, cols], w_sem.at[t, k])

    for k in range(SIDE):
        for t in range(4):
            w_copy(t, k).start()

    barrier = pltpu.get_barrier_semaphore()

    @pl.loop(1, NODES)
    def _(k):
        pl.semaphore_signal(barrier, inc=1, device_id={"node": lax.rem(n + k, NODES)}, device_id_type=MESH)

    if clusters > 1:
        @pl.loop(1, clusters)
        def _(k):
            pl.semaphore_signal(
                barrier, inc=1, device_id={"clus": lax.rem(c + k, clusters)}, device_id_type=MESH
            )

    row_id = lax.broadcasted_iota(jnp.int32, (EIG, EIG), 0)
    col_id = lax.broadcasted_iota(jnp.int32, (EIG, EIG), 1)
    lam = jnp.sum(jnp.where(row_id == col_id, lam_ref[...], 0.0), axis=1, keepdims=True)
    kt[64:128, :] = (lam * eig_ref[...].astype(F32)).astype(BF16)
    kt[144:256, :] = jnp.zeros((112, NC), BF16)
    bias = jnp.where(mask_ref[...] > 0, 0.0, ABSENT)
    for j in range(NODES):
        kt[128:144, j * TOK : (j + 1) * TOK] = jnp.broadcast_to(bias[:, j : j + 1], (16, TOK)).astype(BF16)
        eig_part = eig_ref[:, j * TOK : (j + 1) * TOK].astype(F32)
        full = jnp.concatenate([jnp.zeros((64, TOK), F32), eig_part], axis=0)
        eigt[j * TOK : (j + 1) * TOK, :] = full.T.astype(BF16)
    eqt[64:128, :] = eig_ref[...]

    for load in loads:
        load.wait()
    pl.semaphore_wait(barrier, NODES - 1 + clusters - 1)

    def copy_to(src, dst, send_sem, recv_sem, node):
        return pltpu.make_async_remote_copy(
            src_ref=src, dst_ref=dst, send_sem=send_sem, recv_sem=recv_sem,
            device_id={"node": node}, device_id_type=MESH,
        )

    def along_x(x):
        return x * SIDE + my

    def along_y(y):
        return mx * SIDE + y

    rings = []
    for buf, at, to in ((xlx, mx, along_x), (xly, my, along_y), (cly, my, along_y)):
        before, after, far = turn(at, 3), turn(at, 1), turn(at, 2)
        rings.append((
            ((0, buf.at[at], buf.at[before], to(after)), (1, buf.at[at], buf.at[after], to(before))),
            ((2, buf.at[before, pl.ds(0, 64)], buf.at[far, pl.ds(0, 64)], to(after)),
             (3, buf.at[after, pl.ds(64, 64)], buf.at[far, pl.ds(64, 64)], to(before))),
        ))

    def ring(which, stage, action):
        for number, out, into, node in rings[which][stage]:
            sems = ring_send.at[which, number], ring_recv.at[which, number]
            if action == "start":
                copy_to(out, out, *sems, node).start()
            elif action == "recv":
                copy_to(into, into, *sems, node).wait_recv()
            else:
                copy_to(out, out, *sems, node).wait_send()

    ring(0, 0, "start")
    ring(1, 0, "start")

    low = lax.broadcasted_iota(jnp.int32, (TOK, 128), 1) < 64

    def forward(t):
        return copy_to(send.at[t], recv.at[n], f_send.at[t], f_recv.at[n], t)

    def forward_self():
        return pltpu.make_async_copy(send.at[n], recv.at[n], f_recv.at[n])

    for k in range(SIDE):
        first = turn(mx, k) * SIDE
        cols = pl.ds(pl.multiple_of(first * HS, 256), 256)
        rows_x = xly[my]
        parts = []
        for t in range(4):
            w_copy(t, k).wait()
            product = dot(rows_x if t < 3 else cly[my], w[t, :, cols])
            parts.append(product * SCALE if t == 0 else product)
        for pair in range(2):
            q, kk, v, d = (a[:, pair * 128 : (pair + 1) * 128] for a in parts)
            qs, ks, vs, ds = (pltpu.roll(a, 64, 1) for a in (q, kk, v, d))
            t0 = first + 2 * pair
            send[t0, :, 0:128] = jnp.where(low, q, ds).astype(BF16)
            send[t0, :, 128:256] = jnp.where(low, kk, vs).astype(BF16)
            send[t0 + 1, :, 0:128] = jnp.where(low, qs, d).astype(BF16)
            send[t0 + 1, :, 128:256] = jnp.where(low, ks, v).astype(BF16)
        for j in range(SIDE):
            t = first + j

            @pl.when(t != n)
            def _():
                forward(t).start()

            @pl.when(t == n)
            def _():
                forward_self().start()

    acc_k[...] = jnp.zeros_like(acc_k)
    acc_v[...] = jnp.zeros_like(acc_v)

    @pl.loop(0, NODES)
    def _(k):
        s = lax.rem(n + k, NODES)

        @pl.when(s != n)
        def _():
            copy_to(recv.at[s], recv.at[s], f_send.at[s], f_recv.at[s], s).wait_recv()

        @pl.when(s == n)
        def _():
            forward_self().wait()

        rows = pl.ds(pl.multiple_of(s * TOK, TOK), TOK)
        a = recv[s, :, 0:128].astype(F32)
        b = recv[s, :, 128:256].astype(F32)
        e = eigt[rows, :].astype(F32)
        qe[rows, :] = jnp.where(low, a, e).astype(BF16)
        ke[rows, :] = jnp.where(low, b, e).astype(BF16)
        d0[rows, :] = jnp.where(low, 0.0, a).astype(BF16)
        bm[rows, :] = b.astype(BF16)
        at = a.T.astype(BF16)
        b_t = b.T.astype(BF16)
        eqt[0:64, rows] = at[0:64]
        dt[:, rows] = at[64:128]
        kt[0:64, rows] = b_t[0:64]
        bt[:, rows] = b_t

    ring(0, 0, "recv")
    ring(1, 0, "recv")
    ring(2, 0, "start")
    ring(0, 1, "start")
    ring(1, 1, "start")

    def early(t, which):
        tx, ty = lax.div(t, SIDE), lax.rem(t, SIDE)
        if which == 0:
            return grads.at[tx, ty, 1], ha.at[tx, 0, my], along_y(ty)
        return grads.at[tx, ty, 4], hb.at[ty, 1, mx], along_x(tx)

    def early_start(t):
        for which in range(2):
            src, dst, node = early(t, which)

            @pl.when(node != n)
            def _():
                slot = lax.div(t, SIDE) * SIDE + my if which == 0 else lax.rem(t, SIDE) * SIDE + mx
                copy_to(src, dst, e_send.at[which, t], e_recv.at[which, slot], node).start()

            @pl.when(node == n)
            def _():
                slot = lax.div(t, SIDE) * SIDE + my if which == 0 else lax.rem(t, SIDE) * SIDE + mx
                pltpu.make_async_copy(src, dst, e_recv.at[which, slot]).start()

    def early_recv(which):
        @pl.loop(0, NODES)
        def _(slot):
            group, head = lax.div(slot, SIDE), lax.rem(slot, SIDE)
            own = my if which == 0 else mx
            node = along_y(head) if which == 0 else along_x(head)
            dst = ha.at[group, 0, head] if which == 0 else hb.at[group, 1, head]

            @pl.when(head != own)
            def _():
                copy_to(dst, dst, e_send.at[which, slot], e_recv.at[which, slot], node).wait_recv()

            @pl.when(head == own)
            def _():
                src = grads.at[group, my, 1] if which == 0 else grads.at[mx, group, 4]
                pltpu.make_async_copy(src, dst, e_recv.at[which, slot]).wait()

    def early_sent(which):
        @pl.loop(0, NODES)
        def _(t):
            src, dst, node = early(t, which)

            @pl.when(node != n)
            def _():
                copy_to(src, src, e_send.at[which, t], e_recv.at[which, t], node).wait_send()

    lane = lax.broadcasted_iota(jnp.int32, (ROWS, 128), 1)
    sub = lax.div(lax.broadcasted_iota(jnp.int32, (ROWS, 128), 0), TOK)
    steps = NC // ROWS

    @pl.loop(0, steps)
    def _(i):
        @pl.when(i == steps // 2)
        def _():
            ring(2, 0, "recv")
            ring(2, 1, "start")

        rows = pl.ds(pl.multiple_of(i * ROWS, ROWS), ROWS)
        tile = jnp.where(lane == sub + i * (ROWS // TOK), 1.0, 0.0).astype(BF16)
        scores = dot(jnp.concatenate([qe[rows, :], tile], axis=1), kt[...])
        dprob = dot(d0[rows, :], bt[...])
        raised = jnp.exp(scores - jnp.max(scores, axis=1, keepdims=True))
        inverse = 1.0 / jnp.sum(raised, axis=1, keepdims=True)
        prob = raised * inverse
        delta = jnp.sum(prob * dprob, axis=1, keepdims=True)
        half = prob.astype(BF16)
        dscore = (prob * (dprob - delta)).astype(BF16)
        out = dot(half, bm[...])
        grad_q = dot(dscore, ke[...])
        acc_k[...] += dot(eqt[:, rows], dscore)
        acc_v[...] += dot(dt[:, rows], half)
        grad_qt = grad_q.T
        left[:, rows] = grad_qt[64:128]
        out_t = out.T
        for j in range(ROWS // TOK):
            t = i * (ROWS // TOK) + j
            cols = slice(j * TOK, (j + 1) * TOK)
            tx, ty = lax.div(t, SIDE), lax.rem(t, SIDE)
            grads[tx, ty, 1] = (grad_qt[0:64, cols] * SCALE).astype(BF16)
            grads[tx, ty, 4] = out_t[64:128, cols].astype(BF16)
            early_start(t)

    for t in range(NODES):
        cols = slice(t * TOK, (t + 1) * TOK)
        tx, ty = divmod(t, SIDE)
        grads[tx, ty, 2] = acc_k[0:64, cols].astype(BF16)
        grads[tx, ty, 3] = acc_v[:, cols].astype(BF16)

    def late(which, k, action):
        own = my if which == 0 else mx
        j = turn(own, k)
        node = along_y(j) if which == 0 else along_x(j)
        if which == 0:
            src, dst, into = grads.at[:, j, 2], ha.at[:, 1, my], ha.at[:, 1, j]
        else:
            src, dst, into = grads.at[j, :, 3], hb.at[:, 0, mx], hb.at[:, 0, j]
        if k == 0:
            move = pltpu.make_async_copy(src, dst, l_recv.at[which, own])
            if action == "start":
                move.start()
            elif action == "recv":
                move.wait()
        elif action == "start":
            copy_to(src, dst, l_send.at[which, j], l_recv.at[which, own], node).start()
        elif action == "recv":
            copy_to(into, into, l_send.at[which, j], l_recv.at[which, j], node).wait_recv()
        else:
            copy_to(src, src, l_send.at[which, j], l_recv.at[which, own], node).wait_send()

    def lines(kind, k, action):
        own = my if kind < 2 else mx
        j = turn(own, k)
        node = along_y(j) if kind < 2 else along_x(j)
        sems = p_send.at[kind, j]
        if k == 0:
            move = pltpu.make_async_copy(part.at[kind, own], sums.at[kind, own], p_recv.at[kind, own])
            if action == "start":
                move.start()
            elif action == "recv":
                move.wait()
        elif action == "start":
            copy_to(part.at[kind, j], sums.at[kind, own], sems, p_recv.at[kind, own], node).start()
        elif action == "recv":
            copy_to(sums.at[kind, j], sums.at[kind, j], sems, p_recv.at[kind, j], node).wait_recv()
        else:
            copy_to(part.at[kind, j], part.at[kind, j], sems, p_recv.at[kind, own], node).wait_send()

    for which in range(2):
        for k in (2, 1, 3, 0):
            late(which, k, "start")

    left_all = left[...]
    eig_terms = (lam * (left_all + acc_k[64:128])).astype(BF16)
    for t in range(NODES):
        tx, ty = divmod(t, SIDE)
        grads[tx, ty, 0] = eig_terms[:, t * TOK : (t + 1) * TOK]

    def multiply(kind):
        buf, index, rows_in = ((ha, 0, xlx), (ha, 1, xlx), (hb, 0, xly), (hb, 1, cly))[kind]
        lhs = jnp.concatenate([buf[g, index].reshape(SIDE * HS, TOK) for g in range(SIDE)], axis=1)
        product = dot(lhs, rows_in[...].reshape(SIDE * TOK, D))
        part[kind] = product.astype(BF16).reshape(SIDE, HS, D)
        for k in (2, 1, 3, 0):
            lines(kind, k, "start")

    for which in range(3):
        if which == 2:
            ring(2, 1, "recv")
        else:
            ring(which, 1, "recv")
    early_recv(0)
    multiply(0)
    early_recv(1)
    multiply(3)
    for which in range(2):
        for k in range(SIDE):
            late(which, k, "recv")
        multiply(1 + which)

    def backward(t):
        return copy_to(
            grads.at[lax.div(t, SIDE), lax.rem(t, SIDE), pl.ds(0, 4)], landed(n), b_send.at[t], b_recv.at[n], t
        )

    def landed(s):
        return back.at[:, pl.ds(pl.multiple_of(s * HS, HS), HS), :]

    def backward_self():
        return pltpu.make_async_copy(grads.at[mx, my, pl.ds(0, 4)], landed(n), b_recv.at[n])

    backward_self().start()

    @pl.loop(1, NODES)
    def _(k):
        backward(lax.rem(n + k, NODES)).start()

    weight_col = jnp.sum(eig_ref[...].astype(F32) * left_all, axis=1, keepdims=True)
    row_w = lax.broadcasted_iota(jnp.int32, (EIG, 256), 0)
    col_w = lax.broadcasted_iota(jnp.int32, (EIG, 256), 1)
    weight_row = jnp.sum(jnp.where(row_w == col_w, weight_col, 0.0), axis=0, keepdims=True)
    weight_high = weight_row.astype(BF16).astype(F32)
    row_g = lax.broadcasted_iota(jnp.int32, (16, 256), 0)
    weight_part = jnp.where(
        row_g == 0, weight_high, jnp.where(row_g == 1, weight_row - weight_high, 0.0)
    ).astype(BF16)

    for kind in (0, 3, 1, 2):
        for k in range(SIDE):
            lines(kind, k, "recv")

    def across(t):
        return pltpu.make_async_remote_copy(
            src_ref=gs.at[t], dst_ref=gr.at[c], send_sem=c_send.at[t], recv_sem=c_recv.at[c],
            device_id={"clus": t}, device_id_type=MESH,
        )

    def across_in(s):
        return pltpu.make_async_remote_copy(
            src_ref=gr.at[s], dst_ref=gr.at[s], send_sem=c_send.at[s], recv_sem=c_recv.at[s],
            device_id={"clus": s}, device_id_type=MESH,
        )

    def across_self():
        return pltpu.make_async_copy(gs.at[c], gr.at[c], c_recv.at[c])

    for m in range(4):
        cols = slice(m * 256, (m + 1) * 256)
        stacked = []
        for kind in range(4):
            total = sums[kind, 0, :, cols].astype(F32)
            for j in range(1, SIDE):
                total += sums[kind, j, :, cols].astype(F32)
            stacked.append(total)
        g = jnp.concatenate(stacked, axis=0).T.astype(BF16)
        size = min(chunk, 256)
        for piece in range(256 // size):
            owner, lo = divmod(m * 256 + piece * size, chunk)
            gs[owner, lo : lo + size, :] = g[piece * size : (piece + 1) * size]
            if lo + size == chunk:
                gs[owner, chunk : chunk + 16, :] = weight_part

                @pl.when(c != owner)
                def _():
                    across(owner).start()

                @pl.when(c == owner)
                def _():
                    across_self().start()

    backward_self().wait()

    @pl.loop(1, NODES)
    def _(k):
        s = lax.rem(n + k, NODES)
        copy_to(landed(s), landed(s), b_send.at[s], b_recv.at[s], s).wait_recv()

    for m in range(4):
        rows = slice(m * 256, (m + 1) * 256)
        total = dot(w[0, rows, :], back[1]) + dot(w[1, rows, :], back[2]) + dot(w[2, rows, :], back[3])
        gn_ref[:, rows] = total.T.astype(BF16)
    eig_total = back[0, 0:64, :].astype(F32)
    for s in range(1, NODES):
        eig_total += back[0, s * 64 : (s + 1) * 64, :].astype(F32)
    ge_ref[...] = eig_total

    across_self().wait()
    if clusters > 1:
        @pl.loop(1, clusters)
        def _(k):
            across_in(lax.rem(c + k, clusters)).wait_recv()

    total = gr[0].astype(F32)
    for s in range(1, clusters):
        total += gr[s].astype(F32)
    for pair in range(2):
        both = total[0:chunk, pair * 128 : (pair + 1) * 128]
        gp_ref[2 * pair] = both[:, 0:64]
        gp_ref[2 * pair + 1] = pltpu.roll(both, 64, 1)[:, 0:64]
    gw_ref[...] = (total[chunk : chunk + 1] + total[chunk + 1 : chunk + 2])[:, 0:64]

    for which in range(3):
        for stage in range(2):
            ring(which, stage, "send")
    for which in range(2):
        early_sent(which)
        for k in range(1, SIDE):
            late(which, k, "sent")
    for kind in range(4):
        for k in range(1, SIDE):
            lines(kind, k, "sent")

    @pl.loop(1, NODES)
    def _(k):
        t = lax.rem(n + k, NODES)
        forward(t).wait_send()
        backward(t).wait_send()

    if clusters > 1:
        @pl.loop(1, clusters)
        def _(k):
            across(lax.rem(c + k, clusters)).wait_send()


def outputs(*refs):
    copies = [pltpu.make_async_copy(refs[i], refs[4 + i], refs[8].at[i]) for i in range(4)]
    for copy in copies:
        copy.start()
    for copy in copies:
        copy.wait()


def body(clusters, node_feats, cotangent, w_query, w_key, w_value, w_out, eigvec, eig_weight, block_mask):
    chunk = D // clusters
    anywhere = pl.BlockSpec(memory_space=pl.ANY)
    vmem = pl.BlockSpec(memory_space=pltpu.VMEM)
    dma = pltpu.SemaphoreType.DMA
    shapes = (
        jax.ShapeDtypeStruct((TOK, D), BF16),
        jax.ShapeDtypeStruct((EIG, TOK), F32),
        jax.ShapeDtypeStruct((1, EIG), F32),
        jax.ShapeDtypeStruct((4, chunk, HS), F32),
    )
    results = pl.pallas_call(
        functools.partial(kernel, clusters),
        out_shape=shapes,
        in_specs=[anywhere] * 6 + [vmem] * 3,
        out_specs=(vmem,) * 4,
        scratch_shapes=[
            pltpu.VMEM((4, D, D), BF16),
            pltpu.VMEM((SIDE, TOK, D), BF16),
            pltpu.VMEM((SIDE, TOK, D), BF16),
            pltpu.VMEM((SIDE, TOK, D), BF16),
            pltpu.VMEM((NODES, TOK, 256), BF16),
            pltpu.VMEM((NODES, TOK, 256), BF16),
            pltpu.VMEM((NC, 128), BF16),
            pltpu.VMEM((NC, 128), BF16),
            pltpu.VMEM((NC, 128), BF16),
            pltpu.VMEM((NC, 128), BF16),
            pltpu.VMEM((NC, 128), BF16),
            pltpu.VMEM((128, NC), BF16),
            pltpu.VMEM((64, NC), BF16),
            pltpu.VMEM((256, NC), BF16),
            pltpu.VMEM((128, NC), BF16),
            pltpu.VMEM((128, NC), F32),
            pltpu.VMEM((64, NC), F32),
            pltpu.VMEM((SIDE, SIDE, 5, HS, TOK), BF16),
            pltpu.VMEM((64, NC), F32),
            pltpu.VMEM((4, D, TOK), BF16),
            pltpu.VMEM((SIDE, 2, SIDE, HS, TOK), BF16),
            pltpu.VMEM((SIDE, 2, SIDE, HS, TOK), BF16),
            pltpu.VMEM((4, SIDE, HS, D), BF16),
            pltpu.VMEM((4, SIDE, HS, D), BF16),
            pltpu.VMEM((clusters, chunk + 16, 256), BF16),
            pltpu.VMEM((clusters, chunk + 16, 256), BF16),
            dma((3,)),
            dma((4, 4)),
            dma((3, 4)),
            dma((3, 4)),
            dma((NODES,)),
            dma((NODES,)),
            dma((NODES,)),
            dma((NODES,)),
            dma((2, NODES)),
            dma((2, NODES)),
            dma((2, SIDE)),
            dma((2, SIDE)),
            dma((4, SIDE)),
            dma((4, SIDE)),
            dma((clusters,)),
            dma((clusters,)),
        ],
        compiler_params=pltpu.CompilerParams(
            collective_id=0, has_side_effects=True, vmem_limit_bytes=60 * 1024 * 1024
        ),
        cost_estimate=pl.CostEstimate(flops=8 * 10**9, bytes_accessed=10**7, transcendentals=4 * 10**6),
    )(
        node_feats[0], cotangent[0], w_query, w_key, w_value, w_out,
        eigvec[0], eig_weight, block_mask[0, 0],
    )
    gn, ge, gw, gp = pl.pallas_call(
        outputs,
        out_shape=shapes,
        in_specs=[anywhere] * 4,
        out_specs=(anywhere,) * 4,
        scratch_shapes=[dma((4,))],
    )(*results)
    return gn[None], ge[None], gw, gp


def solution(mesh):
    placed = (
        P("clus", "node", None),
        P("clus", "node", None),
        P(),
        P(),
        P(),
        P(),
        P("clus", None, None),
        P("node", None),
        P("clus", "node", None, None),
    )
    return jax.shard_map(
        functools.partial(body, mesh.shape["clus"]),
        mesh=mesh,
        in_specs=placed,
        out_specs=(
            P("clus", "node", None),
            P("clus", None, "node"),
            P("node", None),
            P(None, "clus", "node"),
        ),
        check_vma=False,
    )
```

```python
import functools

import jax
import jax.numpy as jnp
from jax import lax
from jax.experimental import pallas as pl
from jax.experimental.pallas import tpu as pltpu
from jax.sharding import PartitionSpec as P

MESH = pl.DeviceIdType.MESH
F32 = jnp.float32
BF16 = jnp.bfloat16
ABSENT = -(2.0**100)
SIDE = 4
NODES = 16
TOK = 128
D = 1024
NC = 2048
EIG = 64
HS = 64
SCALE = HS**-0.5
ROWS = 256


def dot(a, b):
    return lax.dot_general(a, b, (((1,), (0,)), ((), ())), preferred_element_type=F32)


def kernel(
    clusters,
    x_hbm, cot_hbm, wq_hbm, wk_hbm, wv_hbm, wo_hbm, eig_ref, lam_ref, mask_ref,
    gn_ref, ge_ref, gw_ref, gp_ref,
    w, xlx, xly, cly, send, recv, eigt, qe, d0, ke, bm, eqt, dt, kt, bt,
    acc_k, acc_v, grads, left, eigs, back, ha, hb, part, mid, sums, gs, gr,
    in_sem, w_sem, ring_send, ring_recv, f_send, f_recv, b_send, b_recv, e_send, e_recv, l_send, l_recv,
    p_send, p_recv, h_send, h_recv, c_send, c_recv,
):
    n = lax.axis_index("node")
    c = lax.axis_index("clus")
    mx = lax.div(n, SIDE)
    my = lax.rem(n, SIDE)
    chunk = D // clusters

    def turn(i, by):
        return lax.rem(i + by, SIDE)

    loads = [
        pltpu.make_async_copy(x_hbm, xlx.at[mx], in_sem.at[0]),
        pltpu.make_async_copy(x_hbm, xly.at[my], in_sem.at[1]),
        pltpu.make_async_copy(cot_hbm, cly.at[my], in_sem.at[2]),
    ]
    for load in loads:
        load.start()
    w_hbm = (wq_hbm, wk_hbm, wv_hbm, wo_hbm)

    def w_copy(t, k):
        cols = pl.ds(pl.multiple_of(turn(mx, k) * 256, 256), 256)
        return pltpu.make_async_copy(w_hbm[t].at[:, cols], w.at[t, :, cols], w_sem.at[t, k])

    for k in range(SIDE):
        for t in range(4):
            w_copy(t, k).start()

    barrier = pltpu.get_barrier_semaphore()

    @pl.loop(1, NODES)
    def _(k):
        pl.semaphore_signal(barrier, inc=1, device_id={"node": lax.rem(n + k, NODES)}, device_id_type=MESH)

    if clusters > 1:
        @pl.loop(1, clusters)
        def _(k):
            pl.semaphore_signal(
                barrier, inc=1, device_id={"clus": lax.rem(c + k, clusters)}, device_id_type=MESH
            )

    row_id = lax.broadcasted_iota(jnp.int32, (EIG, EIG), 0)
    col_id = lax.broadcasted_iota(jnp.int32, (EIG, EIG), 1)
    lam = jnp.sum(jnp.where(row_id == col_id, lam_ref[...], 0.0), axis=1, keepdims=True)
    kt[64:128, :] = (lam * eig_ref[...].astype(F32)).astype(BF16)
    kt[144:256, :] = jnp.zeros((112, NC), BF16)
    bias = jnp.where(mask_ref[...] > 0, 0.0, ABSENT)
    for j in range(NODES):
        kt[128:144, j * TOK : (j + 1) * TOK] = jnp.broadcast_to(bias[:, j : j + 1], (16, TOK)).astype(BF16)
        eig_part = eig_ref[:, j * TOK : (j + 1) * TOK].astype(F32)
        full = jnp.concatenate([jnp.zeros((64, TOK), F32), eig_part], axis=0)
        eigt[j * TOK : (j + 1) * TOK, :] = full.T.astype(BF16)
    eqt[64:128, :] = eig_ref[...]

    for load in loads:
        load.wait()
    pl.semaphore_wait(barrier, NODES - 1 + clusters - 1)

    def copy_to(src, dst, send_sem, recv_sem, node):
        return pltpu.make_async_remote_copy(
            src_ref=src, dst_ref=dst, send_sem=send_sem, recv_sem=recv_sem,
            device_id={"node": node}, device_id_type=MESH,
        )

    def along_x(x):
        return x * SIDE + my

    def along_y(y):
        return mx * SIDE + y

    rings = []
    for buf, at, to in ((xlx, mx, along_x), (xly, my, along_y), (cly, my, along_y)):
        before, after, far = turn(at, 3), turn(at, 1), turn(at, 2)
        rings.append((
            ((0, buf.at[at], buf.at[before], to(after)), (1, buf.at[at], buf.at[after], to(before))),
            ((2, buf.at[before, pl.ds(0, 64)], buf.at[far, pl.ds(0, 64)], to(after)),
             (3, buf.at[after, pl.ds(64, 64)], buf.at[far, pl.ds(64, 64)], to(before))),
        ))

    def ring(which, stage, action):
        for number, out, into, node in rings[which][stage]:
            sems = ring_send.at[which, number], ring_recv.at[which, number]
            if action == "start":
                copy_to(out, out, *sems, node).start()
            elif action == "recv":
                copy_to(into, into, *sems, node).wait_recv()
            else:
                copy_to(out, out, *sems, node).wait_send()

    ring(0, 0, "start")
    ring(1, 0, "start")

    low = lax.broadcasted_iota(jnp.int32, (TOK, 128), 1) < 64

    def forward(t):
        return copy_to(send.at[t], recv.at[n], f_send.at[t], f_recv.at[n], t)

    def forward_self():
        return pltpu.make_async_copy(send.at[n], recv.at[n], f_recv.at[n])

    for k in range(SIDE):
        first = turn(mx, k) * SIDE
        cols = pl.ds(pl.multiple_of(first * HS, 256), 256)
        rows_x = xly[my]
        parts = []
        for t in range(4):
            w_copy(t, k).wait()
            product = dot(rows_x if t < 3 else cly[my], w[t, :, cols])
            parts.append(product * SCALE if t == 0 else product)
        for pair in range(2):
            q, kk, v, d = (a[:, pair * 128 : (pair + 1) * 128] for a in parts)
            qs, ks, vs, ds = (pltpu.roll(a, 64, 1) for a in (q, kk, v, d))
            t0 = first + 2 * pair
            send[t0, :, 0:128] = jnp.where(low, q, ds).astype(BF16)
            send[t0, :, 128:256] = jnp.where(low, kk, vs).astype(BF16)
            send[t0 + 1, :, 0:128] = jnp.where(low, qs, d).astype(BF16)
            send[t0 + 1, :, 128:256] = jnp.where(low, ks, v).astype(BF16)
        for j in range(SIDE):
            t = first + j

            @pl.when(t != n)
            def _():
                forward(t).start()

            @pl.when(t == n)
            def _():
                forward_self().start()

    acc_k[...] = jnp.zeros_like(acc_k)
    acc_v[...] = jnp.zeros_like(acc_v)

    @pl.loop(0, NODES)
    def _(k):
        s = lax.rem(n + k, NODES)

        @pl.when(s != n)
        def _():
            copy_to(recv.at[s], recv.at[s], f_send.at[s], f_recv.at[s], s).wait_recv()

        @pl.when(s == n)
        def _():
            forward_self().wait()

        rows = pl.ds(pl.multiple_of(s * TOK, TOK), TOK)
        a = recv[s, :, 0:128].astype(F32)
        b = recv[s, :, 128:256].astype(F32)
        e = eigt[rows, :].astype(F32)
        qe[rows, :] = jnp.where(low, a, e).astype(BF16)
        ke[rows, :] = jnp.where(low, b, e).astype(BF16)
        d0[rows, :] = jnp.where(low, 0.0, a).astype(BF16)
        bm[rows, :] = b.astype(BF16)
        at = a.T.astype(BF16)
        b_t = b.T.astype(BF16)
        eqt[0:64, rows] = at[0:64]
        dt[:, rows] = at[64:128]
        kt[0:64, rows] = b_t[0:64]
        bt[:, rows] = b_t

    ring(0, 0, "recv")
    ring(1, 0, "recv")
    ring(2, 0, "start")
    ring(0, 1, "start")
    ring(1, 1, "start")

    def early(t, which):
        tx, ty = lax.div(t, SIDE), lax.rem(t, SIDE)
        if which == 0:
            return grads.at[tx, ty, 1], ha.at[tx, 0, my], along_y(ty)
        return grads.at[tx, ty, 4], hb.at[ty, 1, mx], along_x(tx)

    def early_start(t):
        for which in range(2):
            src, dst, node = early(t, which)

            @pl.when(node != n)
            def _():
                slot = lax.div(t, SIDE) * SIDE + my if which == 0 else lax.rem(t, SIDE) * SIDE + mx
                copy_to(src, dst, e_send.at[which, t], e_recv.at[which, slot], node).start()

            @pl.when(node == n)
            def _():
                slot = lax.div(t, SIDE) * SIDE + my if which == 0 else lax.rem(t, SIDE) * SIDE + mx
                pltpu.make_async_copy(src, dst, e_recv.at[which, slot]).start()

    def early_recv(which):
        @pl.loop(0, NODES)
        def _(slot):
            group, head = lax.div(slot, SIDE), lax.rem(slot, SIDE)
            own = my if which == 0 else mx
            node = along_y(head) if which == 0 else along_x(head)
            dst = ha.at[group, 0, head] if which == 0 else hb.at[group, 1, head]

            @pl.when(head != own)
            def _():
                copy_to(dst, dst, e_send.at[which, slot], e_recv.at[which, slot], node).wait_recv()

            @pl.when(head == own)
            def _():
                src = grads.at[group, my, 1] if which == 0 else grads.at[mx, group, 4]
                pltpu.make_async_copy(src, dst, e_recv.at[which, slot]).wait()

    def early_sent(which):
        @pl.loop(0, NODES)
        def _(t):
            src, dst, node = early(t, which)

            @pl.when(node != n)
            def _():
                copy_to(src, src, e_send.at[which, t], e_recv.at[which, t], node).wait_send()

    lane = lax.broadcasted_iota(jnp.int32, (ROWS, 128), 1)
    sub = lax.div(lax.broadcasted_iota(jnp.int32, (ROWS, 128), 0), TOK)
    steps = NC // ROWS

    @pl.loop(0, steps)
    def _(i):
        @pl.when(i == steps // 2)
        def _():
            ring(2, 0, "recv")
            ring(2, 1, "start")

        rows = pl.ds(pl.multiple_of(i * ROWS, ROWS), ROWS)
        tile = jnp.where(lane == sub + i * (ROWS // TOK), 1.0, 0.0).astype(BF16)
        scores = dot(jnp.concatenate([qe[rows, :], tile], axis=1), kt[...])
        dprob = dot(d0[rows, :], bt[...])
        raised = jnp.exp(scores - jnp.max(scores, axis=1, keepdims=True))
        inverse = 1.0 / jnp.sum(raised, axis=1, keepdims=True)
        prob = raised * inverse
        delta = jnp.sum(prob * dprob, axis=1, keepdims=True)
        half = prob.astype(BF16)
        dscore = (prob * (dprob - delta)).astype(BF16)
        out = dot(half, bm[...])
        grad_q = dot(dscore, ke[...])
        acc_k[...] += dot(eqt[:, rows], dscore)
        acc_v[...] += dot(dt[:, rows], half)
        grad_qt = grad_q.T
        left[:, rows] = grad_qt[64:128]
        out_t = out.T
        for j in range(ROWS // TOK):
            t = i * (ROWS // TOK) + j
            cols = slice(j * TOK, (j + 1) * TOK)
            tx, ty = lax.div(t, SIDE), lax.rem(t, SIDE)
            grads[tx, ty, 1] = (grad_qt[0:64, cols] * SCALE).astype(BF16)
            grads[tx, ty, 4] = out_t[64:128, cols].astype(BF16)
            early_start(t)

    for t in range(NODES):
        cols = slice(t * TOK, (t + 1) * TOK)
        tx, ty = divmod(t, SIDE)
        grads[tx, ty, 2] = acc_k[0:64, cols].astype(BF16)
        grads[tx, ty, 3] = acc_v[:, cols].astype(BF16)

    def late(which, k, action):
        own = my if which == 0 else mx
        j = turn(own, k)
        node = along_y(j) if which == 0 else along_x(j)
        if which == 0:
            src, dst, into = grads.at[:, j, 2], ha.at[:, 1, my], ha.at[:, 1, j]
        else:
            src, dst, into = grads.at[j, :, 3], hb.at[:, 0, mx], hb.at[:, 0, j]
        if k == 0:
            move = pltpu.make_async_copy(src, dst, l_recv.at[which, own])
            if action == "start":
                move.start()
            elif action == "recv":
                move.wait()
        elif action == "start":
            copy_to(src, dst, l_send.at[which, j], l_recv.at[which, own], node).start()
        elif action == "recv":
            copy_to(into, into, l_send.at[which, j], l_recv.at[which, j], node).wait_recv()
        else:
            copy_to(src, src, l_send.at[which, j], l_recv.at[which, own], node).wait_send()

    def lines(kind, stage, action):
        own = my if kind < 2 else mx
        to = along_y if kind < 2 else along_x
        after, far, before = turn(own, 1), turn(own, 2), turn(own, 3)
        for way in range(2):
            if stage == 0:
                src, dst = part.at[kind, far, pl.ds(32 * way, 32)], mid.at[kind, way]
            else:
                src, dst = part.at[kind, before if way else after], sums.at[kind, way]
            number = 2 * stage + way
            move = copy_to(
                src, dst, p_send.at[kind, number], p_recv.at[kind, number], to(before if way else after)
            )
            if action == "start":
                move.start()
            elif action == "recv":
                move.wait_recv()
            else:
                move.wait_send()

    def pass_on(kind):
        lines(kind, 0, "recv")
        own = my if kind < 2 else mx
        for way in range(2):
            rows = pl.ds(32 * way, 32)
            there = turn(own, 3 if way else 1)
            part[kind, there, rows] = (part[kind, there, rows].astype(F32) + mid[kind, way].astype(F32)).astype(BF16)
        lines(kind, 1, "start")

    def onward(kind, k, action):
        own, to = (mx, along_x) if kind < 2 else (my, along_y)
        j = turn(own, k)

        def ends(sent, head):
            if kind < 2:
                return ha.at[sent, kind], back.at[kind, head]
            return hb.at[sent, 0], back.at[kind, :, head]

        src, dst = ends(j, own)
        if k == 0:
            move = pltpu.make_async_copy(src, dst, h_recv.at[kind, own])
            if action == "start":
                move.start()
            elif action == "recv":
                move.wait()
        elif action == "start":
            copy_to(src, dst, h_send.at[kind, j], h_recv.at[kind, own], to(j)).start()
        elif action == "recv":
            into = ends(j, j)[1]
            copy_to(into, into, h_send.at[kind, j], h_recv.at[kind, j], to(j)).wait_recv()
        else:
            copy_to(src, src, h_send.at[kind, j], h_recv.at[kind, own], to(j)).wait_send()

    for which in range(2):
        for k in (2, 1, 3, 0):
            late(which, k, "start")

    left_all = left[...]
    eig_terms = (lam * (left_all + acc_k[64:128])).astype(BF16)
    for t in range(NODES):
        tx, ty = divmod(t, SIDE)
        grads[tx, ty, 0] = eig_terms[:, t * TOK : (t + 1) * TOK]

    def multiply(kind):
        buf, index, rows_in = ((ha, 0, xlx), (ha, 1, xlx), (hb, 0, xly), (hb, 1, cly))[kind]
        lhs = jnp.concatenate([buf[g, index].reshape(SIDE * HS, TOK) for g in range(SIDE)], axis=1)
        product = dot(lhs, rows_in[...].reshape(SIDE * TOK, D))
        part[kind] = product.astype(BF16).reshape(SIDE, HS, D)
        lines(kind, 0, "start")

    for which in range(3):
        if which == 2:
            ring(2, 1, "recv")
        else:
            ring(which, 1, "recv")
    early_recv(0)
    early_recv(1)
    multiply(0)
    multiply(3)
    for k in (2, 1, 3, 0):
        onward(0, k, "start")
    for which in range(2):
        for k in range(SIDE):
            late(which, k, "recv")
    pass_on(0)
    multiply(1)
    pass_on(3)
    multiply(2)
    for kind in (1, 2):
        for k in (2, 1, 3, 0):
            onward(kind, k, "start")
        pass_on(kind)

    def backward(t):
        return copy_to(grads.at[lax.div(t, SIDE), lax.rem(t, SIDE), 0], eigs.at[n], b_send.at[t], b_recv.at[n], t)

    def backward_self():
        return pltpu.make_async_copy(grads.at[mx, my, 0], eigs.at[n], b_recv.at[n])

    backward_self().start()

    @pl.loop(1, NODES)
    def _(k):
        backward(lax.rem(n + k, NODES)).start()

    weight_col = jnp.sum(eig_ref[...].astype(F32) * left_all, axis=1, keepdims=True)
    row_w = lax.broadcasted_iota(jnp.int32, (EIG, 128), 0)
    col_w = lax.broadcasted_iota(jnp.int32, (EIG, 128), 1)
    weight_row = jnp.sum(jnp.where(row_w == col_w, weight_col, 0.0), axis=0, keepdims=True)
    weight_high = weight_row.astype(BF16).astype(F32)
    row_g = lax.broadcasted_iota(jnp.int32, (16, 128), 0)
    weight_part = jnp.where(
        row_g == 0, weight_high, jnp.where(row_g == 1, weight_row - weight_high, 0.0)
    ).astype(BF16)

    def rows_of(group):
        return pl.ds(0, chunk + 16 * group)

    def across(group, t):
        return pltpu.make_async_remote_copy(
            src_ref=gs.at[group, t, rows_of(group)], dst_ref=gr.at[group, c, rows_of(group)],
            send_sem=c_send.at[group, t], recv_sem=c_recv.at[group, c],
            device_id={"clus": t}, device_id_type=MESH,
        )

    def across_in(group, s):
        return pltpu.make_async_remote_copy(
            src_ref=gr.at[group, s, rows_of(group)], dst_ref=gr.at[group, s, rows_of(group)],
            send_sem=c_send.at[group, s], recv_sem=c_recv.at[group, s],
            device_id={"clus": s}, device_id_type=MESH,
        )

    def across_self(group):
        return pltpu.make_async_copy(
            gs.at[group, c, rows_of(group)], gr.at[group, c, rows_of(group)], c_recv.at[group, c]
        )

    for group, kinds in enumerate(((0, 3), (1, 2))):
        for kind in kinds:
            lines(kind, 1, "recv")
        for m in range(4):
            cols = slice(m * 256, (m + 1) * 256)
            stacked = []
            for kind in kinds:
                total = part[kind, my if kind < 2 else mx, :, cols].astype(F32)
                stacked.append(total + sums[kind, 0, :, cols].astype(F32) + sums[kind, 1, :, cols].astype(F32))
            g = jnp.concatenate(stacked, axis=0).T.astype(BF16)
            size = min(chunk, 256)
            for piece in range(256 // size):
                owner, lo = divmod(m * 256 + piece * size, chunk)
                gs[group, owner, lo : lo + size, :] = g[piece * size : (piece + 1) * size]
                if lo + size == chunk and group == 1:
                    gs[group, owner, chunk : chunk + 16, :] = weight_part
        across_self(group).start()
        if clusters > 1:
            @pl.loop(1, clusters)
            def _(k):
                across(group, lax.rem(c + k, clusters)).start()

    for kind in range(3):
        for k in range(SIDE):
            onward(kind, k, "recv")
    for m in range(4):
        rows = slice(m * 256, (m + 1) * 256)
        total = dot(w[0, rows, :], back[0].reshape(D, TOK))
        total += dot(w[1, rows, :], back[1].reshape(D, TOK))
        total += dot(w[2, rows, :], back[2].reshape(D, TOK))
        gn_ref[:, rows] = total.T.astype(BF16)

    backward_self().wait()

    @pl.loop(1, NODES)
    def _(k):
        s = lax.rem(n + k, NODES)
        copy_to(eigs.at[s], eigs.at[s], b_send.at[s], b_recv.at[s], s).wait_recv()

    eig_total = eigs[0].astype(F32)
    for s in range(1, NODES):
        eig_total += eigs[s].astype(F32)
    ge_ref[...] = eig_total

    for group, kinds in enumerate(((0, 3), (1, 2))):
        across_self(group).wait()
        if clusters > 1:
            @pl.loop(1, clusters)
            def _(k):
                across_in(group, lax.rem(c + k, clusters)).wait_recv()

        used = slice(0, chunk + 16 * group)
        total = gr[group, 0, used].astype(F32)
        for s in range(1, clusters):
            total += gr[group, s, used].astype(F32)
        gp_ref[kinds[0]] = total[0:chunk, 0:64]
        gp_ref[kinds[1]] = pltpu.roll(total[0:chunk], 64, 1)[:, 0:64]
        if group == 1:
            gw_ref[...] = (total[chunk : chunk + 1] + total[chunk + 1 : chunk + 2])[:, 0:64]

    for which in range(3):
        for stage in range(2):
            ring(which, stage, "send")
    for which in range(2):
        early_sent(which)
        for k in range(1, SIDE):
            late(which, k, "sent")
    for kind in range(4):
        for stage in range(2):
            lines(kind, stage, "sent")
    for kind in range(3):
        for k in range(1, SIDE):
            onward(kind, k, "sent")

    @pl.loop(1, NODES)
    def _(k):
        t = lax.rem(n + k, NODES)
        forward(t).wait_send()
        backward(t).wait_send()

    if clusters > 1:
        @pl.loop(1, clusters)
        def _(k):
            across(0, lax.rem(c + k, clusters)).wait_send()
            across(1, lax.rem(c + k, clusters)).wait_send()


def outputs(*refs):
    for i in range(4):
        refs[4 + i][...] = refs[i][...]


def body(clusters, node_feats, cotangent, w_query, w_key, w_value, w_out, eigvec, eig_weight, block_mask):
    chunk = D // clusters
    anywhere = pl.BlockSpec(memory_space=pl.ANY)
    vmem = pl.BlockSpec(memory_space=pltpu.VMEM)
    dma = pltpu.SemaphoreType.DMA
    shapes = (
        jax.ShapeDtypeStruct((TOK, D), BF16),
        jax.ShapeDtypeStruct((EIG, TOK), F32),
        jax.ShapeDtypeStruct((1, EIG), F32),
        jax.ShapeDtypeStruct((4, chunk, HS), F32),
    )
    results = pl.pallas_call(
        functools.partial(kernel, clusters),
        out_shape=shapes,
        in_specs=[anywhere] * 6 + [vmem] * 3,
        out_specs=(vmem,) * 4,
        scratch_shapes=[
            pltpu.VMEM((4, D, D), BF16),
            pltpu.VMEM((SIDE, TOK, D), BF16),
            pltpu.VMEM((SIDE, TOK, D), BF16),
            pltpu.VMEM((SIDE, TOK, D), BF16),
            pltpu.VMEM((NODES, TOK, 256), BF16),
            pltpu.VMEM((NODES, TOK, 256), BF16),
            pltpu.VMEM((NC, 128), BF16),
            pltpu.VMEM((NC, 128), BF16),
            pltpu.VMEM((NC, 128), BF16),
            pltpu.VMEM((NC, 128), BF16),
            pltpu.VMEM((NC, 128), BF16),
            pltpu.VMEM((128, NC), BF16),
            pltpu.VMEM((64, NC), BF16),
            pltpu.VMEM((256, NC), BF16),
            pltpu.VMEM((128, NC), BF16),
            pltpu.VMEM((128, NC), F32),
            pltpu.VMEM((64, NC), F32),
            pltpu.VMEM((SIDE, SIDE, 5, HS, TOK), BF16),
            pltpu.VMEM((64, NC), F32),
            pltpu.VMEM((NODES, EIG, TOK), BF16),
            pltpu.VMEM((3, SIDE, SIDE, HS, TOK), BF16),
            pltpu.VMEM((SIDE, 2, SIDE, HS, TOK), BF16),
            pltpu.VMEM((SIDE, 2, SIDE, HS, TOK), BF16),
            pltpu.VMEM((4, SIDE, HS, D), BF16),
            pltpu.VMEM((4, 2, HS // 2, D), BF16),
            pltpu.VMEM((4, 2, HS, D), BF16),
            pltpu.VMEM((2, clusters, chunk + 16, 128), BF16),
            pltpu.VMEM((2, clusters, chunk + 16, 128), BF16),
            dma((3,)),
            dma((4, 4)),
            dma((3, 4)),
            dma((3, 4)),
            dma((NODES,)),
            dma((NODES,)),
            dma((NODES,)),
            dma((NODES,)),
            dma((2, NODES)),
            dma((2, NODES)),
            dma((2, SIDE)),
            dma((2, SIDE)),
            dma((4, SIDE)),
            dma((4, SIDE)),
            dma((3, SIDE)),
            dma((3, SIDE)),
            dma((2, clusters)),
            dma((2, clusters)),
        ],
        compiler_params=pltpu.CompilerParams(
            collective_id=0, has_side_effects=True, vmem_limit_bytes=60 * 1024 * 1024
        ),
        cost_estimate=pl.CostEstimate(flops=8 * 10**9, bytes_accessed=10**7, transcendentals=4 * 10**6),
    )(
        node_feats[0], cotangent[0], w_query, w_key, w_value, w_out,
        eigvec[0], eig_weight, block_mask[0, 0],
    )
    gn, ge, gw, gp = pl.pallas_call(
        outputs,
        out_shape=shapes,
        in_specs=[vmem] * 4,
        out_specs=(vmem,) * 4,
    )(*results)
    return gn[None], ge[None], gw, gp


def solution(mesh):
    placed = (
        P("clus", "node", None),
        P("clus", "node", None),
        P(),
        P(),
        P(),
        P(),
        P("clus", None, None),
        P("node", None),
        P("clus", "node", None, None),
    )
    return jax.shard_map(
        functools.partial(body, mesh.shape["clus"]),
        mesh=mesh,
        in_specs=placed,
        out_specs=(
            P("clus", "node", None),
            P("clus", None, "node"),
            P("node", None),
            P(None, "clus", "node"),
        ),
        check_vma=False,
    )
```

```python
import functools

import jax
import jax.numpy as jnp
from jax import lax
from jax.experimental import pallas as pl
from jax.experimental.pallas import tpu as pltpu
from jax.sharding import PartitionSpec as P

MESH = pl.DeviceIdType.MESH
F32 = jnp.float32
BF16 = jnp.bfloat16
ABSENT = -(2.0**100)
SIDE = 4
NODES = 16
TOK = 128
D = 1024
NC = 2048
EIG = 64
HS = 64
SCALE = HS**-0.5
ROWS = 256


def dot(a, b):
    return lax.dot_general(a, b, (((1,), (0,)), ((), ())), preferred_element_type=F32)


def kernel(
    clusters,
    x_hbm, cot_hbm, wq_hbm, wk_hbm, wv_hbm, wo_hbm, eig_ref, lam_ref, mask_ref,
    gn_ref, ge_ref, gw_ref, gp_ref,
    w, xlx, xly, cly, send, recv, eigt, qe, d0, ke, bm, eqt, dt, kt, bt,
    acc_k, acc_v, grads, left, eigs, back, ha, hb, part, mid, sums, gs, gr,
    in_sem, w_sem, ring_send, ring_recv, f_send, f_recv, b_send, b_recv, o_send, o_recv, q_send, q_recv, l_send, l_recv,
    p_send, p_recv, h_send, h_recv, c_send, c_recv,
):
    n = lax.axis_index("node")
    c = lax.axis_index("clus")
    mx = lax.div(n, SIDE)
    my = lax.rem(n, SIDE)
    chunk = D // clusters

    def turn(i, by):
        return lax.rem(i + by, SIDE)

    loads = [
        pltpu.make_async_copy(x_hbm, xlx.at[mx], in_sem.at[0]),
        pltpu.make_async_copy(x_hbm, xly.at[my], in_sem.at[1]),
        pltpu.make_async_copy(cot_hbm, cly.at[my], in_sem.at[2]),
    ]
    for load in loads:
        load.start()
    w_hbm = (wq_hbm, wk_hbm, wv_hbm, wo_hbm)

    def w_copy(t, k):
        cols = pl.ds(pl.multiple_of(turn(mx, k) * 256, 256), 256)
        return pltpu.make_async_copy(w_hbm[t].at[:, cols], w.at[t, :, cols], w_sem.at[t, k])

    for t in range(4):
        w_copy(t, 0).start()

    barrier = pltpu.get_barrier_semaphore()

    @pl.loop(1, NODES)
    def _(k):
        pl.semaphore_signal(barrier, inc=1, device_id={"node": lax.rem(n + k, NODES)}, device_id_type=MESH)

    if clusters > 1:
        @pl.loop(1, clusters)
        def _(k):
            pl.semaphore_signal(
                barrier, inc=1, device_id={"clus": lax.rem(c + k, clusters)}, device_id_type=MESH
            )

    row_id = lax.broadcasted_iota(jnp.int32, (EIG, EIG), 0)
    col_id = lax.broadcasted_iota(jnp.int32, (EIG, EIG), 1)
    lam = jnp.sum(jnp.where(row_id == col_id, lam_ref[...], 0.0), axis=1, keepdims=True)
    kt[64:128, :] = (lam * eig_ref[...].astype(F32)).astype(BF16)
    kt[144:256, :] = jnp.zeros((112, NC), BF16)
    bias = jnp.where(mask_ref[...] > 0, 0.0, ABSENT)
    for j in range(NODES):
        kt[128:144, j * TOK : (j + 1) * TOK] = jnp.broadcast_to(bias[:, j : j + 1], (16, TOK)).astype(BF16)
        eig_part = eig_ref[:, j * TOK : (j + 1) * TOK].astype(F32)
        full = jnp.concatenate([jnp.zeros((64, TOK), F32), eig_part], axis=0)
        eigt[j * TOK : (j + 1) * TOK, :] = full.T.astype(BF16)
    eqt[64:128, :] = eig_ref[...]

    for load in loads:
        load.wait()
    pl.semaphore_wait(barrier, NODES - 1 + clusters - 1)

    def copy_to(src, dst, send_sem, recv_sem, node):
        return pltpu.make_async_remote_copy(
            src_ref=src, dst_ref=dst, send_sem=send_sem, recv_sem=recv_sem,
            device_id={"node": node}, device_id_type=MESH,
        )

    def along_x(x):
        return x * SIDE + my

    def along_y(y):
        return mx * SIDE + y

    rings = []
    for buf, at, to in ((xlx, mx, along_x), (xly, my, along_y), (cly, my, along_y)):
        before, after, far = turn(at, 3), turn(at, 1), turn(at, 2)
        rings.append((
            ((0, buf.at[at], buf.at[before], to(after)), (1, buf.at[at], buf.at[after], to(before))),
            ((2, buf.at[before, pl.ds(0, 64)], buf.at[far, pl.ds(0, 64)], to(after)),
             (3, buf.at[after, pl.ds(64, 64)], buf.at[far, pl.ds(64, 64)], to(before))),
        ))

    def ring(which, stage, action):
        for number, out, into, node in rings[which][stage]:
            sems = ring_send.at[which, number], ring_recv.at[which, number]
            if action == "start":
                copy_to(out, out, *sems, node).start()
            elif action == "recv":
                copy_to(into, into, *sems, node).wait_recv()
            else:
                copy_to(out, out, *sems, node).wait_send()

    ring(0, 0, "start")
    ring(1, 0, "start")

    low = lax.broadcasted_iota(jnp.int32, (TOK, 128), 1) < 64

    def forward(t):
        return copy_to(send.at[t], recv.at[n], f_send.at[t], f_recv.at[n], t)

    def forward_self():
        return pltpu.make_async_copy(send.at[n], recv.at[n], f_recv.at[n])

    for k in range(SIDE):
        first = turn(mx, k) * SIDE
        cols = pl.ds(pl.multiple_of(first * HS, 256), 256)
        rows_x = xly[my]
        parts = []
        for t in range(4):
            w_copy(t, k).wait()
            if k + 1 < SIDE:
                w_copy(t, k + 1).start()
            product = dot(rows_x if t < 3 else cly[my], w[t, :, cols])
            parts.append(product * SCALE if t == 0 else product)
        for pair in range(2):
            q, kk, v, d = (a[:, pair * 128 : (pair + 1) * 128] for a in parts)
            qs, ks, vs, ds = (pltpu.roll(a, 64, 1) for a in (q, kk, v, d))
            t0 = first + 2 * pair
            send[t0, :, 0:128] = jnp.where(low, q, ds).astype(BF16)
            send[t0, :, 128:256] = jnp.where(low, kk, vs).astype(BF16)
            send[t0 + 1, :, 0:128] = jnp.where(low, qs, d).astype(BF16)
            send[t0 + 1, :, 128:256] = jnp.where(low, ks, v).astype(BF16)
        for j in range(SIDE):
            t = first + j

            @pl.when(t != n)
            def _():
                forward(t).start()

            @pl.when(t == n)
            def _():
                forward_self().start()

    acc_k[...] = jnp.zeros_like(acc_k)
    acc_v[...] = jnp.zeros_like(acc_v)

    @pl.loop(0, NODES)
    def _(k):
        s = lax.rem(n + k, NODES)

        @pl.when(s != n)
        def _():
            copy_to(recv.at[s], recv.at[s], f_send.at[s], f_recv.at[s], s).wait_recv()

        @pl.when(s == n)
        def _():
            forward_self().wait()

        rows = pl.ds(pl.multiple_of(s * TOK, TOK), TOK)
        a = recv[s, :, 0:128].astype(F32)
        b = recv[s, :, 128:256].astype(F32)
        e = eigt[rows, :].astype(F32)
        qe[rows, :] = jnp.where(low, a, e).astype(BF16)
        ke[rows, :] = jnp.where(low, b, e).astype(BF16)
        d0[rows, :] = jnp.where(low, 0.0, a).astype(BF16)
        bm[rows, :] = b.astype(BF16)
        at = a.T.astype(BF16)
        b_t = b.T.astype(BF16)
        eqt[0:64, rows] = at[0:64]
        dt[:, rows] = at[64:128]
        kt[0:64, rows] = b_t[0:64]
        bt[:, rows] = b_t

    ring(0, 0, "recv")
    ring(1, 0, "recv")
    ring(2, 0, "start")
    ring(0, 1, "start")
    ring(1, 1, "start")

    def early_output(tx):
        src, dst = grads.at[tx, :, 4], hb.at[:, 1, mx]

        @pl.when(tx != mx)
        def _():
            copy_to(src, dst, o_send.at[tx], o_recv.at[mx], along_x(tx)).start()

        @pl.when(tx == mx)
        def _():
            pltpu.make_async_copy(src, dst, o_recv.at[mx]).start()

    def early_output_wait(k, action):
        j = turn(mx, k)
        into = hb.at[:, 1, j]
        if k == 0:
            if action == "recv":
                pltpu.make_async_copy(grads.at[mx, :, 4], into, o_recv.at[mx]).wait()
        elif action == "recv":
            copy_to(into, into, o_send.at[j], o_recv.at[j], along_x(j)).wait_recv()
        else:
            src = grads.at[j, :, 4]
            copy_to(src, src, o_send.at[j], o_recv.at[mx], along_x(j)).wait_send()

    def early_query(half, k, action):
        j = turn(my, k)
        groups = pl.ds(2 * half, 2)
        src, dst, into = grads.at[groups, j, 1], ha.at[groups, 0, my], ha.at[groups, 0, j]
        if k == 0:
            move = pltpu.make_async_copy(src, dst, q_recv.at[half, my])
            if action == "start":
                move.start()
            elif action == "recv":
                move.wait()
        elif action == "start":
            copy_to(src, dst, q_send.at[half, j], q_recv.at[half, my], along_y(j)).start()
        elif action == "recv":
            copy_to(into, into, q_send.at[half, j], q_recv.at[half, j], along_y(j)).wait_recv()
        else:
            copy_to(src, src, q_send.at[half, j], q_recv.at[half, my], along_y(j)).wait_send()

    lane = lax.broadcasted_iota(jnp.int32, (ROWS, 128), 1)
    sub = lax.div(lax.broadcasted_iota(jnp.int32, (ROWS, 128), 0), TOK)
    steps = NC // ROWS

    @pl.loop(0, steps)
    def _(i):
        @pl.when(i == steps // 2)
        def _():
            ring(2, 0, "recv")
            ring(2, 1, "start")

        rows = pl.ds(pl.multiple_of(i * ROWS, ROWS), ROWS)
        tile = jnp.where(lane == sub + i * (ROWS // TOK), 1.0, 0.0).astype(BF16)
        scores = dot(jnp.concatenate([qe[rows, :], tile], axis=1), kt[...])
        dprob = dot(d0[rows, :], bt[...])
        raised = jnp.exp(scores - jnp.max(scores, axis=1, keepdims=True))
        inverse = 1.0 / jnp.sum(raised, axis=1, keepdims=True)
        prob = raised * inverse
        delta = jnp.sum(prob * dprob, axis=1, keepdims=True)
        half = prob.astype(BF16)
        dscore = (prob * (dprob - delta)).astype(BF16)
        out = dot(half, bm[...])
        grad_q = dot(dscore, ke[...])
        acc_k[...] += dot(eqt[:, rows], dscore)
        acc_v[...] += dot(dt[:, rows], half)
        grad_qt = grad_q.T
        left[:, rows] = grad_qt[64:128]
        out_t = out.T
        for j in range(ROWS // TOK):
            t = i * (ROWS // TOK) + j
            cols = slice(j * TOK, (j + 1) * TOK)
            tx, ty = lax.div(t, SIDE), lax.rem(t, SIDE)
            grads[tx, ty, 1] = (grad_qt[0:64, cols] * SCALE).astype(BF16)
            grads[tx, ty, 4] = out_t[64:128, cols].astype(BF16)

        @pl.when(lax.rem(i, 2) == 1)
        def _():
            early_output(lax.div(i, 2))

        @pl.when(i == steps // 2 - 1)
        def _():
            for k in (2, 1, 3, 0):
                early_query(0, k, "start")

    for k in (2, 1, 3, 0):
        early_query(1, k, "start")
    for t in range(NODES):
        cols = slice(t * TOK, (t + 1) * TOK)
        tx, ty = divmod(t, SIDE)
        grads[tx, ty, 2] = acc_k[0:64, cols].astype(BF16)
        grads[tx, ty, 3] = acc_v[:, cols].astype(BF16)

    def late(which, k, action):
        own = my if which == 0 else mx
        j = turn(own, k)
        node = along_y(j) if which == 0 else along_x(j)
        if which == 0:
            src, dst, into = grads.at[:, j, 2], ha.at[:, 1, my], ha.at[:, 1, j]
        else:
            src, dst, into = grads.at[j, :, 3], hb.at[:, 0, mx], hb.at[:, 0, j]
        if k == 0:
            move = pltpu.make_async_copy(src, dst, l_recv.at[which, own])
            if action == "start":
                move.start()
            elif action == "recv":
                move.wait()
        elif action == "start":
            copy_to(src, dst, l_send.at[which, j], l_recv.at[which, own], node).start()
        elif action == "recv":
            copy_to(into, into, l_send.at[which, j], l_recv.at[which, j], node).wait_recv()
        else:
            copy_to(src, src, l_send.at[which, j], l_recv.at[which, own], node).wait_send()

    def lines(kind, stage, action):
        own = my if kind < 2 else mx
        to = along_y if kind < 2 else along_x
        after, far, before = turn(own, 1), turn(own, 2), turn(own, 3)
        for way in range(2):
            if stage == 0:
                src, dst = part.at[kind, far, pl.ds(32 * way, 32)], mid.at[kind, way]
            else:
                src, dst = part.at[kind, before if way else after], sums.at[kind, way]
            number = 2 * stage + way
            move = copy_to(
                src, dst, p_send.at[kind, number], p_recv.at[kind, number], to(before if way else after)
            )
            if action == "start":
                move.start()
            elif action == "recv":
                move.wait_recv()
            else:
                move.wait_send()

    def pass_on(kind):
        lines(kind, 0, "recv")
        own = my if kind < 2 else mx
        for way in range(2):
            rows = pl.ds(32 * way, 32)
            there = turn(own, 3 if way else 1)
            part[kind, there, rows] = (part[kind, there, rows].astype(F32) + mid[kind, way].astype(F32)).astype(BF16)
        lines(kind, 1, "start")

    def onward(kind, k, action):
        own, to = (mx, along_x) if kind < 2 else (my, along_y)
        j = turn(own, k)

        def ends(sent, head):
            if kind < 2:
                return ha.at[sent, kind], back.at[kind, head]
            return hb.at[sent, 0], back.at[kind, :, head]

        src, dst = ends(j, own)
        if k == 0:
            move = pltpu.make_async_copy(src, dst, h_recv.at[kind, own])
            if action == "start":
                move.start()
            elif action == "recv":
                move.wait()
        elif action == "start":
            copy_to(src, dst, h_send.at[kind, j], h_recv.at[kind, own], to(j)).start()
        elif action == "recv":
            into = ends(j, j)[1]
            copy_to(into, into, h_send.at[kind, j], h_recv.at[kind, j], to(j)).wait_recv()
        else:
            copy_to(src, src, h_send.at[kind, j], h_recv.at[kind, own], to(j)).wait_send()

    for which in range(2):
        for k in (2, 1, 3, 0):
            late(which, k, "start")

    left_all = left[...]
    eig_terms = (lam * (left_all + acc_k[64:128])).astype(BF16)
    for t in range(NODES):
        tx, ty = divmod(t, SIDE)
        grads[tx, ty, 0] = eig_terms[:, t * TOK : (t + 1) * TOK]

    def multiply(kind):
        buf, index, rows_in = ((ha, 0, xlx), (ha, 1, xlx), (hb, 0, xly), (hb, 1, cly))[kind]
        lhs = jnp.concatenate([buf[g, index].reshape(SIDE * HS, TOK) for g in range(SIDE)], axis=1)
        product = dot(lhs, rows_in[...].reshape(SIDE * TOK, D))
        part[kind] = product.astype(BF16).reshape(SIDE, HS, D)
        lines(kind, 0, "start")

    for which in range(3):
        if which == 2:
            ring(2, 1, "recv")
        else:
            ring(which, 1, "recv")
    for k in range(SIDE):
        early_query(0, k, "recv")
        early_query(1, k, "recv")
        early_output_wait(k, "recv")
    multiply(0)
    multiply(3)
    for k in (2, 1, 3, 0):
        onward(0, k, "start")
    for which in range(2):
        for k in range(SIDE):
            late(which, k, "recv")
    pass_on(0)
    multiply(1)
    pass_on(3)
    multiply(2)
    for kind in (1, 2):
        for k in (2, 1, 3, 0):
            onward(kind, k, "start")
        pass_on(kind)

    def backward(t):
        return copy_to(grads.at[lax.div(t, SIDE), lax.rem(t, SIDE), 0], eigs.at[n], b_send.at[t], b_recv.at[n], t)

    def backward_self():
        return pltpu.make_async_copy(grads.at[mx, my, 0], eigs.at[n], b_recv.at[n])

    backward_self().start()

    @pl.loop(1, NODES)
    def _(k):
        backward(lax.rem(n + k, NODES)).start()

    weight_col = jnp.sum(eig_ref[...].astype(F32) * left_all, axis=1, keepdims=True)
    row_w = lax.broadcasted_iota(jnp.int32, (EIG, 128), 0)
    col_w = lax.broadcasted_iota(jnp.int32, (EIG, 128), 1)
    weight_row = jnp.sum(jnp.where(row_w == col_w, weight_col, 0.0), axis=0, keepdims=True)
    weight_high = weight_row.astype(BF16).astype(F32)
    row_g = lax.broadcasted_iota(jnp.int32, (16, 128), 0)
    weight_part = jnp.where(
        row_g == 0, weight_high, jnp.where(row_g == 1, weight_row - weight_high, 0.0)
    ).astype(BF16)

    def rows_of(group):
        return pl.ds(0, chunk + 16 * group)

    def across(group, t):
        return pltpu.make_async_remote_copy(
            src_ref=gs.at[group, t, rows_of(group)], dst_ref=gr.at[group, c, rows_of(group)],
            send_sem=c_send.at[group, t], recv_sem=c_recv.at[group, c],
            device_id={"clus": t}, device_id_type=MESH,
        )

    def across_in(group, s):
        return pltpu.make_async_remote_copy(
            src_ref=gr.at[group, s, rows_of(group)], dst_ref=gr.at[group, s, rows_of(group)],
            send_sem=c_send.at[group, s], recv_sem=c_recv.at[group, s],
            device_id={"clus": s}, device_id_type=MESH,
        )

    def across_self(group):
        return pltpu.make_async_copy(
            gs.at[group, c, rows_of(group)], gr.at[group, c, rows_of(group)], c_recv.at[group, c]
        )

    for group, kinds in enumerate(((0, 3), (1, 2))):
        for kind in kinds:
            lines(kind, 1, "recv")
        for m in range(4):
            cols = slice(m * 256, (m + 1) * 256)
            stacked = []
            for kind in kinds:
                total = part[kind, my if kind < 2 else mx, :, cols].astype(F32)
                stacked.append(total + sums[kind, 0, :, cols].astype(F32) + sums[kind, 1, :, cols].astype(F32))
            g = jnp.concatenate(stacked, axis=0).T.astype(BF16)
            size = min(chunk, 256)
            for piece in range(256 // size):
                owner, lo = divmod(m * 256 + piece * size, chunk)
                gs[group, owner, lo : lo + size, :] = g[piece * size : (piece + 1) * size]
                if lo + size == chunk and group == 1:
                    gs[group, owner, chunk : chunk + 16, :] = weight_part
        across_self(group).start()
        if clusters > 1:
            @pl.loop(1, clusters)
            def _(k):
                across(group, lax.rem(c + k, clusters)).start()

    for kind in range(3):
        for k in range(SIDE):
            onward(kind, k, "recv")
    for m in range(4):
        rows = slice(m * 256, (m + 1) * 256)
        total = dot(w[0, rows, :], back[0].reshape(D, TOK))
        total += dot(w[1, rows, :], back[1].reshape(D, TOK))
        total += dot(w[2, rows, :], back[2].reshape(D, TOK))
        gn_ref[:, rows] = total.T.astype(BF16)

    backward_self().wait()

    @pl.loop(1, NODES)
    def _(k):
        s = lax.rem(n + k, NODES)
        copy_to(eigs.at[s], eigs.at[s], b_send.at[s], b_recv.at[s], s).wait_recv()

    eig_total = eigs[0].astype(F32)
    for s in range(1, NODES):
        eig_total += eigs[s].astype(F32)
    ge_ref[...] = eig_total

    for group, kinds in enumerate(((0, 3), (1, 2))):
        across_self(group).wait()
        if clusters > 1:
            @pl.loop(1, clusters)
            def _(k):
                across_in(group, lax.rem(c + k, clusters)).wait_recv()

        used = slice(0, chunk + 16 * group)
        total = gr[group, 0, used].astype(F32)
        for s in range(1, clusters):
            total += gr[group, s, used].astype(F32)
        gp_ref[kinds[0]] = total[0:chunk, 0:64]
        gp_ref[kinds[1]] = pltpu.roll(total[0:chunk], 64, 1)[:, 0:64]
        if group == 1:
            gw_ref[...] = (total[chunk : chunk + 1] + total[chunk + 1 : chunk + 2])[:, 0:64]

    for which in range(3):
        for stage in range(2):
            ring(which, stage, "send")
    for which in range(2):
        for k in range(1, SIDE):
            early_query(which, k, "sent")
            if which == 0:
                early_output_wait(k, "sent")
            late(which, k, "sent")
    for kind in range(4):
        for stage in range(2):
            lines(kind, stage, "sent")
    for kind in range(3):
        for k in range(1, SIDE):
            onward(kind, k, "sent")

    @pl.loop(1, NODES)
    def _(k):
        t = lax.rem(n + k, NODES)
        forward(t).wait_send()
        backward(t).wait_send()

    if clusters > 1:
        @pl.loop(1, clusters)
        def _(k):
            across(0, lax.rem(c + k, clusters)).wait_send()
            across(1, lax.rem(c + k, clusters)).wait_send()


def outputs(*refs):
    for i in range(4):
        refs[4 + i][...] = refs[i][...]


def body(clusters, node_feats, cotangent, w_query, w_key, w_value, w_out, eigvec, eig_weight, block_mask):
    chunk = D // clusters
    anywhere = pl.BlockSpec(memory_space=pl.ANY)
    vmem = pl.BlockSpec(memory_space=pltpu.VMEM)
    dma = pltpu.SemaphoreType.DMA
    shapes = (
        jax.ShapeDtypeStruct((TOK, D), BF16),
        jax.ShapeDtypeStruct((EIG, TOK), F32),
        jax.ShapeDtypeStruct((1, EIG), F32),
        jax.ShapeDtypeStruct((4, chunk, HS), F32),
    )
    results = pl.pallas_call(
        functools.partial(kernel, clusters),
        out_shape=shapes,
        in_specs=[anywhere] * 6 + [vmem] * 3,
        out_specs=(vmem,) * 4,
        scratch_shapes=[
            pltpu.VMEM((4, D, D), BF16),
            pltpu.VMEM((SIDE, TOK, D), BF16),
            pltpu.VMEM((SIDE, TOK, D), BF16),
            pltpu.VMEM((SIDE, TOK, D), BF16),
            pltpu.VMEM((NODES, TOK, 256), BF16),
            pltpu.VMEM((NODES, TOK, 256), BF16),
            pltpu.VMEM((NC, 128), BF16),
            pltpu.VMEM((NC, 128), BF16),
            pltpu.VMEM((NC, 128), BF16),
            pltpu.VMEM((NC, 128), BF16),
            pltpu.VMEM((NC, 128), BF16),
            pltpu.VMEM((128, NC), BF16),
            pltpu.VMEM((64, NC), BF16),
            pltpu.VMEM((256, NC), BF16),
            pltpu.VMEM((128, NC), BF16),
            pltpu.VMEM((128, NC), F32),
            pltpu.VMEM((64, NC), F32),
            pltpu.VMEM((SIDE, SIDE, 5, HS, TOK), BF16),
            pltpu.VMEM((64, NC), F32),
            pltpu.VMEM((NODES, EIG, TOK), BF16),
            pltpu.VMEM((3, SIDE, SIDE, HS, TOK), BF16),
            pltpu.VMEM((SIDE, 2, SIDE, HS, TOK), BF16),
            pltpu.VMEM((SIDE, 2, SIDE, HS, TOK), BF16),
            pltpu.VMEM((4, SIDE, HS, D), BF16),
            pltpu.VMEM((4, 2, HS // 2, D), BF16),
            pltpu.VMEM((4, 2, HS, D), BF16),
            pltpu.VMEM((2, clusters, chunk + 16, 128), BF16),
            pltpu.VMEM((2, clusters, chunk + 16, 128), BF16),
            dma((3,)),
            dma((4, 4)),
            dma((3, 4)),
            dma((3, 4)),
            dma((NODES,)),
            dma((NODES,)),
            dma((NODES,)),
            dma((NODES,)),
            dma((SIDE,)),
            dma((SIDE,)),
            dma((2, SIDE)),
            dma((2, SIDE)),
            dma((2, SIDE)),
            dma((2, SIDE)),
            dma((4, SIDE)),
            dma((4, SIDE)),
            dma((3, SIDE)),
            dma((3, SIDE)),
            dma((2, clusters)),
            dma((2, clusters)),
        ],
        compiler_params=pltpu.CompilerParams(
            collective_id=0, has_side_effects=True, vmem_limit_bytes=60 * 1024 * 1024
        ),
        cost_estimate=pl.CostEstimate(flops=8 * 10**9, bytes_accessed=10**7, transcendentals=4 * 10**6),
    )(
        node_feats[0], cotangent[0], w_query, w_key, w_value, w_out,
        eigvec[0], eig_weight, block_mask[0, 0],
    )
    gn, ge, gw, gp = pl.pallas_call(
        outputs,
        out_shape=shapes,
        in_specs=[vmem] * 4,
        out_specs=(vmem,) * 4,
    )(*results)
    return gn[None], ge[None], gw, gp


def solution(mesh):
    placed = (
        P("clus", "node", None),
        P("clus", "node", None),
        P(),
        P(),
        P(),
        P(),
        P("clus", None, None),
        P("node", None),
        P("clus", "node", None, None),
    )
    return jax.shard_map(
        functools.partial(body, mesh.shape["clus"]),
        mesh=mesh,
        in_specs=placed,
        out_specs=(
            P("clus", "node", None),
            P("clus", None, "node"),
            P("node", None),
            P(None, "clus", "node"),
        ),
        check_vma=False,
    )
```

```python
import functools

import jax
import jax.numpy as jnp
from jax import lax
from jax.experimental import pallas as pl
from jax.experimental.pallas import tpu as pltpu
from jax.sharding import PartitionSpec as P

MESH = pl.DeviceIdType.MESH
F32 = jnp.float32
BF16 = jnp.bfloat16
ABSENT = -(2.0**100)
SIDE = 4
NODES = 16
TOK = 128
D = 1024
NC = 2048
EIG = 64
HS = 64
SCALE = HS**-0.5
ROWS = 256


def dot(a, b):
    return lax.dot_general(a, b, (((1,), (0,)), ((), ())), preferred_element_type=F32)


def kernel(
    clusters,
    x_hbm, cot_hbm, wq_hbm, wk_hbm, wv_hbm, wo_hbm, eig_ref, lam_ref, mask_ref,
    gn_ref, ge_ref, gw_ref, gp_ref,
    w, xlx, xly, cly, send, recv, eigt, qe, d0, ke, bm, eqt, dt, kt, bt,
    acc_k, acc_v, grads, left, eigs, back, ha, hb, part, mid, sums, gs, gx, gr,
    in_sem, w_sem, ring_send, ring_recv, f_send, f_recv, b_send, b_recv, o_send, o_recv, q_send, q_recv, l_send, l_recv,
    p_send, p_recv, h_send, h_recv, x_send, x_recv, c_send, c_recv,
):
    n = lax.axis_index("node")
    c = lax.axis_index("clus")
    mx = lax.div(n, SIDE)
    my = lax.rem(n, SIDE)
    chunk = D // clusters
    cores = 2 if clusters % 2 == 0 else 1
    chips = clusters // cores
    chip, core = lax.div(c, cores), lax.rem(c, cores)

    def turn(i, by):
        return lax.rem(i + by, SIDE)

    loads = [
        pltpu.make_async_copy(x_hbm, xlx.at[mx], in_sem.at[0]),
        pltpu.make_async_copy(x_hbm, xly.at[my], in_sem.at[1]),
        pltpu.make_async_copy(cot_hbm, cly.at[my], in_sem.at[2]),
    ]
    for load in loads:
        load.start()
    w_hbm = (wq_hbm, wk_hbm, wv_hbm, wo_hbm)

    def w_copy(t, k):
        cols = pl.ds(pl.multiple_of(turn(mx, k) * 256, 256), 256)
        return pltpu.make_async_copy(w_hbm[t].at[:, cols], w.at[t, :, cols], w_sem.at[t, k])

    for t in range(4):
        w_copy(t, 0).start()

    barrier = pltpu.get_barrier_semaphore()

    @pl.loop(1, NODES)
    def _(k):
        pl.semaphore_signal(barrier, inc=1, device_id={"node": lax.rem(n + k, NODES)}, device_id_type=MESH)

    if clusters > 1:
        @pl.loop(1, clusters)
        def _(k):
            pl.semaphore_signal(
                barrier, inc=1, device_id={"clus": lax.rem(c + k, clusters)}, device_id_type=MESH
            )

    row_id = lax.broadcasted_iota(jnp.int32, (EIG, EIG), 0)
    col_id = lax.broadcasted_iota(jnp.int32, (EIG, EIG), 1)
    lam = jnp.sum(jnp.where(row_id == col_id, lam_ref[...], 0.0), axis=1, keepdims=True)
    kt[64:128, :] = (lam * eig_ref[...].astype(F32)).astype(BF16)
    kt[144:256, :] = jnp.zeros((112, NC), BF16)
    bias = jnp.where(mask_ref[...] > 0, 0.0, ABSENT)
    for j in range(NODES):
        kt[128:144, j * TOK : (j + 1) * TOK] = jnp.broadcast_to(bias[:, j : j + 1], (16, TOK)).astype(BF16)
        eig_part = eig_ref[:, j * TOK : (j + 1) * TOK].astype(F32)
        full = jnp.concatenate([jnp.zeros((64, TOK), F32), eig_part], axis=0)
        eigt[j * TOK : (j + 1) * TOK, :] = full.T.astype(BF16)
    eqt[64:128, :] = eig_ref[...]

    for load in loads:
        load.wait()
    pl.semaphore_wait(barrier, NODES - 1 + clusters - 1)

    def copy_to(src, dst, send_sem, recv_sem, node):
        return pltpu.make_async_remote_copy(
            src_ref=src, dst_ref=dst, send_sem=send_sem, recv_sem=recv_sem,
            device_id={"node": node}, device_id_type=MESH,
        )

    def along_x(x):
        return x * SIDE + my

    def along_y(y):
        return mx * SIDE + y

    rings = []
    for buf, at, to in ((xlx, mx, along_x), (xly, my, along_y), (cly, my, along_y)):
        before, after, far = turn(at, 3), turn(at, 1), turn(at, 2)
        rings.append((
            ((0, buf.at[at], buf.at[before], to(after)), (1, buf.at[at], buf.at[after], to(before))),
            ((2, buf.at[before, pl.ds(0, 64)], buf.at[far, pl.ds(0, 64)], to(after)),
             (3, buf.at[after, pl.ds(64, 64)], buf.at[far, pl.ds(64, 64)], to(before))),
        ))

    def ring(which, stage, action):
        for number, out, into, node in rings[which][stage]:
            sems = ring_send.at[which, number], ring_recv.at[which, number]
            if action == "start":
                copy_to(out, out, *sems, node).start()
            elif action == "recv":
                copy_to(into, into, *sems, node).wait_recv()
            else:
                copy_to(out, out, *sems, node).wait_send()

    ring(0, 0, "start")
    ring(1, 0, "start")

    low = lax.broadcasted_iota(jnp.int32, (TOK, 128), 1) < 64

    def forward(t):
        return copy_to(send.at[t], recv.at[n], f_send.at[t], f_recv.at[n], t)

    def forward_self():
        return pltpu.make_async_copy(send.at[n], recv.at[n], f_recv.at[n])

    for k in range(SIDE):
        first = turn(mx, k) * SIDE
        cols = pl.ds(pl.multiple_of(first * HS, 256), 256)
        rows_x = xly[my]
        parts = []
        for t in range(4):
            w_copy(t, k).wait()
            if k + 1 < SIDE:
                w_copy(t, k + 1).start()
            product = dot(rows_x if t < 3 else cly[my], w[t, :, cols])
            parts.append(product * SCALE if t == 0 else product)
        for pair in range(2):
            q, kk, v, d = (a[:, pair * 128 : (pair + 1) * 128] for a in parts)
            qs, ks, vs, ds = (pltpu.roll(a, 64, 1) for a in (q, kk, v, d))
            t0 = first + 2 * pair
            send[t0, :, 0:128] = jnp.where(low, q, ds).astype(BF16)
            send[t0, :, 128:256] = jnp.where(low, kk, vs).astype(BF16)
            send[t0 + 1, :, 0:128] = jnp.where(low, qs, d).astype(BF16)
            send[t0 + 1, :, 128:256] = jnp.where(low, ks, v).astype(BF16)
        for j in range(SIDE):
            t = first + j

            @pl.when(t != n)
            def _():
                forward(t).start()

            @pl.when(t == n)
            def _():
                forward_self().start()

    acc_k[...] = jnp.zeros_like(acc_k)
    acc_v[...] = jnp.zeros_like(acc_v)

    @pl.loop(0, NODES)
    def _(k):
        s = lax.rem(n + k, NODES)

        @pl.when(s != n)
        def _():
            copy_to(recv.at[s], recv.at[s], f_send.at[s], f_recv.at[s], s).wait_recv()

        @pl.when(s == n)
        def _():
            forward_self().wait()

        rows = pl.ds(pl.multiple_of(s * TOK, TOK), TOK)
        a = recv[s, :, 0:128].astype(F32)
        b = recv[s, :, 128:256].astype(F32)
        e = eigt[rows, :].astype(F32)
        qe[rows, :] = jnp.where(low, a, e).astype(BF16)
        ke[rows, :] = jnp.where(low, b, e).astype(BF16)
        d0[rows, :] = jnp.where(low, 0.0, a).astype(BF16)
        bm[rows, :] = b.astype(BF16)
        at = a.T.astype(BF16)
        b_t = b.T.astype(BF16)
        eqt[0:64, rows] = at[0:64]
        dt[:, rows] = at[64:128]
        kt[0:64, rows] = b_t[0:64]
        bt[:, rows] = b_t

    ring(0, 0, "recv")
    ring(1, 0, "recv")
    ring(2, 0, "start")
    ring(0, 1, "start")
    ring(1, 1, "start")

    def early_output(tx):
        src, dst = grads.at[tx, :, 4], hb.at[:, 1, mx]

        @pl.when(tx != mx)
        def _():
            copy_to(src, dst, o_send.at[tx], o_recv.at[mx], along_x(tx)).start()

        @pl.when(tx == mx)
        def _():
            pltpu.make_async_copy(src, dst, o_recv.at[mx]).start()

    def early_output_wait(k, action):
        j = turn(mx, k)
        into = hb.at[:, 1, j]
        if k == 0:
            if action == "recv":
                pltpu.make_async_copy(grads.at[mx, :, 4], into, o_recv.at[mx]).wait()
        elif action == "recv":
            copy_to(into, into, o_send.at[j], o_recv.at[j], along_x(j)).wait_recv()
        else:
            src = grads.at[j, :, 4]
            copy_to(src, src, o_send.at[j], o_recv.at[mx], along_x(j)).wait_send()

    def early_query(half, k, action):
        j = turn(my, k)
        groups = pl.ds(2 * half, 2)
        src, dst, into = grads.at[groups, j, 1], ha.at[groups, 0, my], ha.at[groups, 0, j]
        if k == 0:
            move = pltpu.make_async_copy(src, dst, q_recv.at[half, my])
            if action == "start":
                move.start()
            elif action == "recv":
                move.wait()
        elif action == "start":
            copy_to(src, dst, q_send.at[half, j], q_recv.at[half, my], along_y(j)).start()
        elif action == "recv":
            copy_to(into, into, q_send.at[half, j], q_recv.at[half, j], along_y(j)).wait_recv()
        else:
            copy_to(src, src, q_send.at[half, j], q_recv.at[half, my], along_y(j)).wait_send()

    lane = lax.broadcasted_iota(jnp.int32, (ROWS, 128), 1)
    sub = lax.div(lax.broadcasted_iota(jnp.int32, (ROWS, 128), 0), TOK)
    steps = NC // ROWS

    @pl.loop(0, steps)
    def _(i):
        @pl.when(i == steps - 2)
        def _():
            ring(2, 0, "recv")
            ring(2, 1, "start")

        rows = pl.ds(pl.multiple_of(i * ROWS, ROWS), ROWS)
        tile = jnp.where(lane == sub + i * (ROWS // TOK), 1.0, 0.0).astype(BF16)
        scores = dot(jnp.concatenate([qe[rows, :], tile], axis=1), kt[...])
        dprob = dot(d0[rows, :], bt[...])
        raised = jnp.exp(scores - jnp.max(scores, axis=1, keepdims=True))
        inverse = 1.0 / jnp.sum(raised, axis=1, keepdims=True)
        prob = raised * inverse
        delta = jnp.sum(prob * dprob, axis=1, keepdims=True)
        half = prob.astype(BF16)
        dscore = (prob * (dprob - delta)).astype(BF16)
        out = dot(half, bm[...])
        grad_q = dot(dscore, ke[...])
        acc_k[...] += dot(eqt[:, rows], dscore)
        acc_v[...] += dot(dt[:, rows], half)
        grad_qt = grad_q.T
        left[:, rows] = grad_qt[64:128]
        out_t = out.T
        for j in range(ROWS // TOK):
            t = i * (ROWS // TOK) + j
            cols = slice(j * TOK, (j + 1) * TOK)
            tx, ty = lax.div(t, SIDE), lax.rem(t, SIDE)
            grads[tx, ty, 1] = (grad_qt[0:64, cols] * SCALE).astype(BF16)
            grads[tx, ty, 4] = out_t[64:128, cols].astype(BF16)

        @pl.when(lax.rem(i, 2) == 1)
        def _():
            early_output(lax.div(i, 2))

        @pl.when(i == steps // 2 - 1)
        def _():
            for k in (2, 1, 3, 0):
                early_query(0, k, "start")

    for k in (2, 1, 3, 0):
        early_query(1, k, "start")
    for t in range(NODES):
        cols = slice(t * TOK, (t + 1) * TOK)
        tx, ty = divmod(t, SIDE)
        grads[tx, ty, 2] = acc_k[0:64, cols].astype(BF16)
        grads[tx, ty, 3] = acc_v[:, cols].astype(BF16)

    def late(which, k, action):
        own = my if which == 0 else mx
        j = turn(own, k)
        node = along_y(j) if which == 0 else along_x(j)
        if which == 0:
            src, dst, into = grads.at[:, j, 2], ha.at[:, 1, my], ha.at[:, 1, j]
        else:
            src, dst, into = grads.at[j, :, 3], hb.at[:, 0, mx], hb.at[:, 0, j]
        if k == 0:
            move = pltpu.make_async_copy(src, dst, l_recv.at[which, own])
            if action == "start":
                move.start()
            elif action == "recv":
                move.wait()
        elif action == "start":
            copy_to(src, dst, l_send.at[which, j], l_recv.at[which, own], node).start()
        elif action == "recv":
            copy_to(into, into, l_send.at[which, j], l_recv.at[which, j], node).wait_recv()
        else:
            copy_to(src, src, l_send.at[which, j], l_recv.at[which, own], node).wait_send()

    def lines(kind, stage, action):
        own = my if kind < 2 else mx
        to = along_y if kind < 2 else along_x
        after, far, before = turn(own, 1), turn(own, 2), turn(own, 3)
        for way in range(2):
            if stage == 0:
                src, dst = part.at[kind, far, pl.ds(32 * way, 32)], mid.at[kind, way]
            else:
                src, dst = part.at[kind, before if way else after], sums.at[kind, way]
            number = 2 * stage + way
            move = copy_to(
                src, dst, p_send.at[kind, number], p_recv.at[kind, number], to(before if way else after)
            )
            if action == "start":
                move.start()
            elif action == "recv":
                move.wait_recv()
            else:
                move.wait_send()

    def pass_on(kind):
        lines(kind, 0, "recv")
        own = my if kind < 2 else mx
        for way in range(2):
            rows = pl.ds(32 * way, 32)
            there = turn(own, 3 if way else 1)
            part[kind, there, rows] = (part[kind, there, rows].astype(F32) + mid[kind, way].astype(F32)).astype(BF16)
        lines(kind, 1, "start")

    def onward(kind, k, action):
        own, to = (mx, along_x) if kind < 2 else (my, along_y)
        j = turn(own, k)

        def ends(sent, head):
            if kind < 2:
                return ha.at[sent, kind], back.at[kind, head]
            return hb.at[sent, 0], back.at[kind, :, head]

        src, dst = ends(j, own)
        if k == 0:
            move = pltpu.make_async_copy(src, dst, h_recv.at[kind, own])
            if action == "start":
                move.start()
            elif action == "recv":
                move.wait()
        elif action == "start":
            copy_to(src, dst, h_send.at[kind, j], h_recv.at[kind, own], to(j)).start()
        elif action == "recv":
            into = ends(j, j)[1]
            copy_to(into, into, h_send.at[kind, j], h_recv.at[kind, j], to(j)).wait_recv()
        else:
            copy_to(src, src, h_send.at[kind, j], h_recv.at[kind, own], to(j)).wait_send()

    for which in range(2):
        for k in (2, 1, 3, 0):
            late(which, k, "start")

    left_all = left[...]
    eig_terms = (lam * (left_all + acc_k[64:128])).astype(BF16)
    for t in range(NODES):
        tx, ty = divmod(t, SIDE)
        grads[tx, ty, 0] = eig_terms[:, t * TOK : (t + 1) * TOK]

    def multiply(kind):
        buf, index, rows_in = ((ha, 0, xlx), (ha, 1, xlx), (hb, 0, xly), (hb, 1, cly))[kind]
        lhs = jnp.concatenate([buf[g, index].reshape(SIDE * HS, TOK) for g in range(SIDE)], axis=1)
        product = dot(lhs, rows_in[...].reshape(SIDE * TOK, D))
        part[kind] = product.astype(BF16).reshape(SIDE, HS, D)
        lines(kind, 0, "start")

    for which in range(3):
        if which == 2:
            ring(2, 1, "recv")
        else:
            ring(which, 1, "recv")
    for k in range(SIDE):
        early_query(0, k, "recv")
        early_query(1, k, "recv")
        early_output_wait(k, "recv")
    multiply(0)
    multiply(3)
    for k in (2, 1, 3, 0):
        onward(0, k, "start")
    for which in range(2):
        for k in range(SIDE):
            late(which, k, "recv")
    pass_on(0)
    multiply(1)
    pass_on(3)
    multiply(2)
    for kind in (1, 2):
        for k in (2, 1, 3, 0):
            onward(kind, k, "start")
        pass_on(kind)

    def backward(t):
        return copy_to(grads.at[lax.div(t, SIDE), lax.rem(t, SIDE), 0], eigs.at[n], b_send.at[t], b_recv.at[n], t)

    def backward_self():
        return pltpu.make_async_copy(grads.at[mx, my, 0], eigs.at[n], b_recv.at[n])

    backward_self().start()

    @pl.loop(1, NODES)
    def _(k):
        backward(lax.rem(n + k, NODES)).start()

    weight_col = jnp.sum(eig_ref[...].astype(F32) * left_all, axis=1, keepdims=True)
    row_w = lax.broadcasted_iota(jnp.int32, (EIG, 128), 0)
    col_w = lax.broadcasted_iota(jnp.int32, (EIG, 128), 1)
    weight_row = jnp.sum(jnp.where(row_w == col_w, weight_col, 0.0), axis=0, keepdims=True)
    weight_high = weight_row.astype(BF16).astype(F32)
    row_g = lax.broadcasted_iota(jnp.int32, (16, 128), 0)
    weight_part = jnp.where(
        row_g == 0, weight_high, jnp.where(row_g == 1, weight_row - weight_high, 0.0)
    ).astype(BF16)

    def rows_of(group):
        return pl.ds(0, chunk + 16 * group)

    def swap(group):
        return pltpu.make_async_remote_copy(
            src_ref=gs.at[group, :, 1 - core, rows_of(group)], dst_ref=gx.at[group, :, rows_of(group)],
            send_sem=x_send.at[group], recv_sem=x_recv.at[group],
            device_id={"clus": chip * cores + 1 - core}, device_id_type=MESH,
        )

    def across(group, t):
        return pltpu.make_async_remote_copy(
            src_ref=gs.at[group, t, core, rows_of(group)], dst_ref=gr.at[group, chip, rows_of(group)],
            send_sem=c_send.at[group, t], recv_sem=c_recv.at[group, chip],
            device_id={"clus": t * cores + core}, device_id_type=MESH,
        )

    def across_in(group, s):
        return pltpu.make_async_remote_copy(
            src_ref=gr.at[group, s, rows_of(group)], dst_ref=gr.at[group, s, rows_of(group)],
            send_sem=c_send.at[group, s], recv_sem=c_recv.at[group, s],
            device_id={"clus": s * cores + core}, device_id_type=MESH,
        )

    def across_self(group):
        return pltpu.make_async_copy(
            gs.at[group, chip, core, rows_of(group)], gr.at[group, chip, rows_of(group)], c_recv.at[group, chip]
        )

    def across_start(group):
        if cores > 1:
            swap(group).wait_recv()
            for t in range(chips):
                both = gs[group, t, core, 0:chunk].astype(F32) + gx[group, t, 0:chunk].astype(F32)
                gs[group, t, core, 0:chunk] = both.astype(BF16)
            if group == 1:
                pair = gs[1, 0, core, chunk : chunk + 16].astype(F32) + gx[1, 0, chunk : chunk + 16].astype(F32)
                weight_sum = jnp.sum(pair, axis=0, keepdims=True)
                weight_top = weight_sum.astype(BF16).astype(F32)
                weight_both = jnp.where(
                    row_g == 0, weight_top, jnp.where(row_g == 1, weight_sum - weight_top, 0.0)
                ).astype(BF16)
                for t in range(chips):
                    gs[1, t, core, chunk : chunk + 16] = weight_both
        across_self(group).start()
        if chips > 1:
            @pl.loop(1, chips)
            def _(k):
                across(group, lax.rem(chip + k, chips)).start()

    for group, kinds in enumerate(((0, 3), (1, 2))):
        for kind in kinds:
            lines(kind, 1, "recv")
        for m in range(4):
            cols = slice(m * 256, (m + 1) * 256)
            stacked = []
            for kind in kinds:
                total = part[kind, my if kind < 2 else mx, :, cols].astype(F32)
                stacked.append(total + sums[kind, 0, :, cols].astype(F32) + sums[kind, 1, :, cols].astype(F32))
            g = jnp.concatenate(stacked, axis=0).T.astype(BF16)
            size = min(chunk, 256)
            for piece in range(256 // size):
                owner, lo = divmod(m * 256 + piece * size, chunk)
                gs[group, owner // cores, owner % cores, lo : lo + size, :] = g[piece * size : (piece + 1) * size]
                if lo + size == chunk and group == 1:
                    gs[group, owner // cores, owner % cores, chunk : chunk + 16, :] = weight_part
        if cores > 1:
            swap(group).start()
    across_start(0)
    across_start(1)

    for kind in range(3):
        for k in range(SIDE):
            onward(kind, k, "recv")
    for m in range(4):
        rows = slice(m * 256, (m + 1) * 256)
        total = dot(w[0, rows, :], back[0].reshape(D, TOK))
        total += dot(w[1, rows, :], back[1].reshape(D, TOK))
        total += dot(w[2, rows, :], back[2].reshape(D, TOK))
        gn_ref[:, rows] = total.T.astype(BF16)

    backward_self().wait()

    @pl.loop(1, NODES)
    def _(k):
        s = lax.rem(n + k, NODES)
        copy_to(eigs.at[s], eigs.at[s], b_send.at[s], b_recv.at[s], s).wait_recv()

    eig_total = eigs[0].astype(F32)
    for s in range(1, NODES):
        eig_total += eigs[s].astype(F32)
    ge_ref[...] = eig_total

    for group, kinds in enumerate(((0, 3), (1, 2))):
        across_self(group).wait()
        if chips > 1:
            @pl.loop(1, chips)
            def _(k):
                across_in(group, lax.rem(chip + k, chips)).wait_recv()

        used = slice(0, chunk + 16 * group)
        total = gr[group, 0, used].astype(F32)
        for s in range(1, chips):
            total += gr[group, s, used].astype(F32)
        gp_ref[kinds[0]] = total[0:chunk, 0:64]
        gp_ref[kinds[1]] = pltpu.roll(total[0:chunk], 64, 1)[:, 0:64]
        if group == 1:
            gw_ref[...] = (total[chunk : chunk + 1] + total[chunk + 1 : chunk + 2])[:, 0:64]

    for which in range(3):
        for stage in range(2):
            ring(which, stage, "send")
    for which in range(2):
        for k in range(1, SIDE):
            early_query(which, k, "sent")
            if which == 0:
                early_output_wait(k, "sent")
            late(which, k, "sent")
    for kind in range(4):
        for stage in range(2):
            lines(kind, stage, "sent")
    for kind in range(3):
        for k in range(1, SIDE):
            onward(kind, k, "sent")

    @pl.loop(1, NODES)
    def _(k):
        t = lax.rem(n + k, NODES)
        forward(t).wait_send()
        backward(t).wait_send()

    if cores > 1:
        swap(0).wait_send()
        swap(1).wait_send()
    if chips > 1:
        @pl.loop(1, chips)
        def _(k):
            across(0, lax.rem(chip + k, chips)).wait_send()
            across(1, lax.rem(chip + k, chips)).wait_send()


def outputs(*refs):
    for i in range(4):
        refs[4 + i][...] = refs[i][...]


def body(clusters, node_feats, cotangent, w_query, w_key, w_value, w_out, eigvec, eig_weight, block_mask):
    chunk = D // clusters
    cores = 2 if clusters % 2 == 0 else 1
    chips = clusters // cores
    anywhere = pl.BlockSpec(memory_space=pl.ANY)
    vmem = pl.BlockSpec(memory_space=pltpu.VMEM)
    dma = pltpu.SemaphoreType.DMA
    shapes = (
        jax.ShapeDtypeStruct((TOK, D), BF16),
        jax.ShapeDtypeStruct((EIG, TOK), F32),
        jax.ShapeDtypeStruct((1, EIG), F32),
        jax.ShapeDtypeStruct((4, chunk, HS), F32),
    )
    results = pl.pallas_call(
        functools.partial(kernel, clusters),
        out_shape=shapes,
        in_specs=[anywhere] * 6 + [vmem] * 3,
        out_specs=(vmem,) * 4,
        scratch_shapes=[
            pltpu.VMEM((4, D, D), BF16),
            pltpu.VMEM((SIDE, TOK, D), BF16),
            pltpu.VMEM((SIDE, TOK, D), BF16),
            pltpu.VMEM((SIDE, TOK, D), BF16),
            pltpu.VMEM((NODES, TOK, 256), BF16),
            pltpu.VMEM((NODES, TOK, 256), BF16),
            pltpu.VMEM((NC, 128), BF16),
            pltpu.VMEM((NC, 128), BF16),
            pltpu.VMEM((NC, 128), BF16),
            pltpu.VMEM((NC, 128), BF16),
            pltpu.VMEM((NC, 128), BF16),
            pltpu.VMEM((128, NC), BF16),
            pltpu.VMEM((64, NC), BF16),
            pltpu.VMEM((256, NC), BF16),
            pltpu.VMEM((128, NC), BF16),
            pltpu.VMEM((128, NC), F32),
            pltpu.VMEM((64, NC), F32),
            pltpu.VMEM((SIDE, SIDE, 5, HS, TOK), BF16),
            pltpu.VMEM((64, NC), F32),
            pltpu.VMEM((NODES, EIG, TOK), BF16),
            pltpu.VMEM((3, SIDE, SIDE, HS, TOK), BF16),
            pltpu.VMEM((SIDE, 2, SIDE, HS, TOK), BF16),
            pltpu.VMEM((SIDE, 2, SIDE, HS, TOK), BF16),
            pltpu.VMEM((4, SIDE, HS, D), BF16),
            pltpu.VMEM((4, 2, HS // 2, D), BF16),
            pltpu.VMEM((4, 2, HS, D), BF16),
            pltpu.VMEM((2, chips, cores, chunk + 16, 128), BF16),
            pltpu.VMEM((2, chips, chunk + 16, 128), BF16),
            pltpu.VMEM((2, chips, chunk + 16, 128), BF16),
            dma((3,)),
            dma((4, 4)),
            dma((3, 4)),
            dma((3, 4)),
            dma((NODES,)),
            dma((NODES,)),
            dma((NODES,)),
            dma((NODES,)),
            dma((SIDE,)),
            dma((SIDE,)),
            dma((2, SIDE)),
            dma((2, SIDE)),
            dma((2, SIDE)),
            dma((2, SIDE)),
            dma((4, SIDE)),
            dma((4, SIDE)),
            dma((3, SIDE)),
            dma((3, SIDE)),
            dma((2,)),
            dma((2,)),
            dma((2, chips)),
            dma((2, chips)),
        ],
        compiler_params=pltpu.CompilerParams(
            collective_id=0, has_side_effects=True, vmem_limit_bytes=60 * 1024 * 1024
        ),
        cost_estimate=pl.CostEstimate(flops=8 * 10**9, bytes_accessed=10**7, transcendentals=4 * 10**6),
    )(
        node_feats[0], cotangent[0], w_query, w_key, w_value, w_out,
        eigvec[0], eig_weight, block_mask[0, 0],
    )
    gn, ge, gw, gp = pl.pallas_call(
        outputs,
        out_shape=shapes,
        in_specs=[vmem] * 4,
        out_specs=(vmem,) * 4,
    )(*results)
    return gn[None], ge[None], gw, gp


def solution(mesh):
    placed = (
        P("clus", "node", None),
        P("clus", "node", None),
        P(),
        P(),
        P(),
        P(),
        P("clus", None, None),
        P("node", None),
        P("clus", "node", None, None),
    )
    return jax.shard_map(
        functools.partial(body, mesh.shape["clus"]),
        mesh=mesh,
        in_specs=placed,
        out_specs=(
            P("clus", "node", None),
            P("clus", None, "node"),
            P("node", None),
            P(None, "clus", "node"),
        ),
        check_vma=False,
    )
```

```python
import functools

import jax
import jax.numpy as jnp
from jax import lax
from jax.experimental import pallas as pl
from jax.experimental.pallas import tpu as pltpu
from jax.sharding import PartitionSpec as P

MESH = pl.DeviceIdType.MESH
F32 = jnp.float32
BF16 = jnp.bfloat16
ABSENT = -(2.0**100)
SIDE = 4
NODES = 16
TOK = 128
D = 1024
NC = 2048
EIG = 64
HS = 64
SCALE = HS**-0.5
ROWS = 512


def dot(a, b):
    return lax.dot_general(a, b, (((1,), (0,)), ((), ())), preferred_element_type=F32)


def kernel(
    clusters,
    x_hbm, cot_hbm, wq_hbm, wk_hbm, wv_hbm, wo_hbm, eig_ref, lam_ref, mask_ref,
    gn_ref, ge_ref, gw_ref, gp_ref,
    w, xlx, xly, cly, send, recv, eigt, qe, d0, ke, bm, eqt, dt, kt, bt,
    acc_k, acc_v, grads, left, eigs, back, ha, hb, part, mid, sums, gs, gx, gr,
    in_sem, w_sem, ring_send, ring_recv, f_send, f_recv, b_send, b_recv, o_send, o_recv, q_send, q_recv, l_send, l_recv,
    p_send, p_recv, h_send, h_recv, x_send, x_recv, c_send, c_recv,
):
    n = lax.axis_index("node")
    c = lax.axis_index("clus")
    mx = lax.div(n, SIDE)
    my = lax.rem(n, SIDE)
    chunk = D // clusters
    cores = 2 if clusters % 2 == 0 else 1
    chips = clusters // cores
    chip, core = lax.div(c, cores), lax.rem(c, cores)

    def turn(i, by):
        return lax.rem(i + by, SIDE)

    loads = [
        pltpu.make_async_copy(x_hbm, xlx.at[mx], in_sem.at[0]),
        pltpu.make_async_copy(x_hbm, xly.at[my], in_sem.at[1]),
        pltpu.make_async_copy(cot_hbm, cly.at[my], in_sem.at[2]),
    ]
    for load in loads:
        load.start()
    w_hbm = (wq_hbm, wk_hbm, wv_hbm, wo_hbm)

    def w_copy(t, k):
        cols = pl.ds(pl.multiple_of(turn(mx, k) * 256, 256), 256)
        return pltpu.make_async_copy(w_hbm[t].at[:, cols], w.at[t, :, cols], w_sem.at[t, k])

    for t in range(4):
        w_copy(t, 0).start()

    barrier = pltpu.get_barrier_semaphore()

    @pl.loop(1, NODES)
    def _(k):
        pl.semaphore_signal(barrier, inc=1, device_id={"node": lax.rem(n + k, NODES)}, device_id_type=MESH)

    if clusters > 1:
        @pl.loop(1, clusters)
        def _(k):
            pl.semaphore_signal(
                barrier, inc=1, device_id={"clus": lax.rem(c + k, clusters)}, device_id_type=MESH
            )

    row_id = lax.broadcasted_iota(jnp.int32, (EIG, EIG), 0)
    col_id = lax.broadcasted_iota(jnp.int32, (EIG, EIG), 1)
    lam = jnp.sum(jnp.where(row_id == col_id, lam_ref[...], 0.0), axis=1, keepdims=True)
    kt[64:128, :] = (lam * eig_ref[...].astype(F32)).astype(BF16)
    kt[144:256, :] = jnp.zeros((112, NC), BF16)
    bias = jnp.where(mask_ref[...] > 0, 0.0, ABSENT)
    for j in range(NODES):
        kt[128:144, j * TOK : (j + 1) * TOK] = jnp.broadcast_to(bias[:, j : j + 1], (16, TOK)).astype(BF16)
        eig_part = eig_ref[:, j * TOK : (j + 1) * TOK].astype(F32)
        full = jnp.concatenate([jnp.zeros((64, TOK), F32), eig_part], axis=0)
        eigt[j * TOK : (j + 1) * TOK, :] = full.T.astype(BF16)
    eqt[64:128, :] = eig_ref[...]

    for load in loads:
        load.wait()
    pl.semaphore_wait(barrier, NODES - 1 + clusters - 1)

    def copy_to(src, dst, send_sem, recv_sem, node):
        return pltpu.make_async_remote_copy(
            src_ref=src, dst_ref=dst, send_sem=send_sem, recv_sem=recv_sem,
            device_id={"node": node}, device_id_type=MESH,
        )

    def along_x(x):
        return x * SIDE + my

    def along_y(y):
        return mx * SIDE + y

    rings = []
    for buf, at, to in ((xlx, mx, along_x), (xly, my, along_y), (cly, my, along_y)):
        before, after, far = turn(at, 3), turn(at, 1), turn(at, 2)
        rings.append((
            ((0, buf.at[at], buf.at[before], to(after)), (1, buf.at[at], buf.at[after], to(before))),
            ((2, buf.at[before, pl.ds(0, 64)], buf.at[far, pl.ds(0, 64)], to(after)),
             (3, buf.at[after, pl.ds(64, 64)], buf.at[far, pl.ds(64, 64)], to(before))),
        ))

    def ring(which, stage, action):
        for number, out, into, node in rings[which][stage]:
            sems = ring_send.at[which, number], ring_recv.at[which, number]
            if action == "start":
                copy_to(out, out, *sems, node).start()
            elif action == "recv":
                copy_to(into, into, *sems, node).wait_recv()
            else:
                copy_to(out, out, *sems, node).wait_send()

    ring(0, 0, "start")
    ring(1, 0, "start")

    low = lax.broadcasted_iota(jnp.int32, (TOK, 128), 1) < 64

    def forward(t):
        return copy_to(send.at[t], recv.at[n], f_send.at[t], f_recv.at[n], t)

    def forward_self():
        return pltpu.make_async_copy(send.at[n], recv.at[n], f_recv.at[n])

    for k in range(SIDE):
        first = turn(mx, k) * SIDE
        cols = pl.ds(pl.multiple_of(first * HS, 256), 256)
        rows_x = xly[my]
        parts = []
        for t in range(4):
            w_copy(t, k).wait()
            if k + 1 < SIDE:
                w_copy(t, k + 1).start()
            product = dot(rows_x if t < 3 else cly[my], w[t, :, cols])
            parts.append(product * SCALE if t == 0 else product)
        for pair in range(2):
            q, kk, v, d = (a[:, pair * 128 : (pair + 1) * 128] for a in parts)
            qs, ks, vs, ds = (pltpu.roll(a, 64, 1) for a in (q, kk, v, d))
            t0 = first + 2 * pair
            send[t0, :, 0:128] = jnp.where(low, q, ds).astype(BF16)
            send[t0, :, 128:256] = jnp.where(low, kk, vs).astype(BF16)
            send[t0 + 1, :, 0:128] = jnp.where(low, qs, d).astype(BF16)
            send[t0 + 1, :, 128:256] = jnp.where(low, ks, v).astype(BF16)
        for j in range(SIDE):
            t = first + j

            @pl.when(t != n)
            def _():
                forward(t).start()

            @pl.when(t == n)
            def _():
                forward_self().start()

    acc_k[...] = jnp.zeros_like(acc_k)
    acc_v[...] = jnp.zeros_like(acc_v)

    @pl.loop(0, NODES)
    def _(k):
        s = lax.rem(n + k, NODES)

        @pl.when(s != n)
        def _():
            copy_to(recv.at[s], recv.at[s], f_send.at[s], f_recv.at[s], s).wait_recv()

        @pl.when(s == n)
        def _():
            forward_self().wait()

        rows = pl.ds(pl.multiple_of(s * TOK, TOK), TOK)
        a = recv[s, :, 0:128].astype(F32)
        b = recv[s, :, 128:256].astype(F32)
        e = eigt[rows, :].astype(F32)
        qe[rows, :] = jnp.where(low, a, e).astype(BF16)
        ke[rows, :] = jnp.where(low, b, e).astype(BF16)
        d0[rows, :] = jnp.where(low, 0.0, a).astype(BF16)
        bm[rows, :] = b.astype(BF16)
        at = a.T.astype(BF16)
        b_t = b.T.astype(BF16)
        eqt[0:64, rows] = at[0:64]
        dt[:, rows] = at[64:128]
        kt[0:64, rows] = b_t[0:64]
        bt[:, rows] = b_t

    ring(0, 0, "recv")
    ring(1, 0, "recv")
    ring(2, 0, "start")
    ring(0, 1, "start")
    ring(1, 1, "start")

    def early_output(tx):
        src, dst = grads.at[tx, :, 4], hb.at[:, 1, mx]

        @pl.when(tx != mx)
        def _():
            copy_to(src, dst, o_send.at[tx], o_recv.at[mx], along_x(tx)).start()

        @pl.when(tx == mx)
        def _():
            pltpu.make_async_copy(src, dst, o_recv.at[mx]).start()

    def early_output_wait(k, action):
        j = turn(mx, k)
        into = hb.at[:, 1, j]
        if k == 0:
            if action == "recv":
                pltpu.make_async_copy(grads.at[mx, :, 4], into, o_recv.at[mx]).wait()
        elif action == "recv":
            copy_to(into, into, o_send.at[j], o_recv.at[j], along_x(j)).wait_recv()
        else:
            src = grads.at[j, :, 4]
            copy_to(src, src, o_send.at[j], o_recv.at[mx], along_x(j)).wait_send()

    def early_query(half, k, action):
        j = turn(my, k)
        groups = pl.ds(2 * half, 2)
        src, dst, into = grads.at[groups, j, 1], ha.at[groups, 0, my], ha.at[groups, 0, j]
        if k == 0:
            move = pltpu.make_async_copy(src, dst, q_recv.at[half, my])
            if action == "start":
                move.start()
            elif action == "recv":
                move.wait()
        elif action == "start":
            copy_to(src, dst, q_send.at[half, j], q_recv.at[half, my], along_y(j)).start()
        elif action == "recv":
            copy_to(into, into, q_send.at[half, j], q_recv.at[half, j], along_y(j)).wait_recv()
        else:
            copy_to(src, src, q_send.at[half, j], q_recv.at[half, my], along_y(j)).wait_send()

    lane = lax.broadcasted_iota(jnp.int32, (ROWS, 128), 1)
    sub = lax.div(lax.broadcasted_iota(jnp.int32, (ROWS, 128), 0), TOK)
    steps = NC // ROWS

    @pl.loop(0, steps)
    def _(i):
        @pl.when(i == steps - 1)
        def _():
            ring(2, 0, "recv")
            ring(2, 1, "start")

        rows = pl.ds(pl.multiple_of(i * ROWS, ROWS), ROWS)
        tile = jnp.where(lane == sub + i * (ROWS // TOK), 1.0, 0.0).astype(BF16)
        scores = dot(jnp.concatenate([qe[rows, :], tile], axis=1), kt[...])
        dprob = dot(d0[rows, :], bt[...])
        raised = jnp.exp(scores - jnp.max(scores, axis=1, keepdims=True))
        inverse = 1.0 / jnp.sum(raised, axis=1, keepdims=True)
        prob = raised * inverse
        delta = jnp.sum(prob * dprob, axis=1, keepdims=True)
        half = prob.astype(BF16)
        dscore = (prob * (dprob - delta)).astype(BF16)
        out = dot(half, bm[...])
        grad_q = dot(dscore, ke[...])
        acc_k[...] += dot(eqt[:, rows], dscore)
        acc_v[...] += dot(dt[:, rows], half)
        grad_qt = grad_q.T
        left[:, rows] = grad_qt[64:128]
        out_t = out.T
        for j in range(ROWS // TOK):
            t = i * (ROWS // TOK) + j
            cols = slice(j * TOK, (j + 1) * TOK)
            tx, ty = lax.div(t, SIDE), lax.rem(t, SIDE)
            grads[tx, ty, 1] = (grad_qt[0:64, cols] * SCALE).astype(BF16)
            grads[tx, ty, 4] = out_t[64:128, cols].astype(BF16)

        early_output(i)

        @pl.when(i == steps // 2 - 1)
        def _():
            for k in (2, 1, 3, 0):
                early_query(0, k, "start")

    for k in (2, 1, 3, 0):
        early_query(1, k, "start")
    for t in range(NODES):
        cols = slice(t * TOK, (t + 1) * TOK)
        tx, ty = divmod(t, SIDE)
        grads[tx, ty, 2] = acc_k[0:64, cols].astype(BF16)
        grads[tx, ty, 3] = acc_v[:, cols].astype(BF16)

    def late(which, k, action):
        own = my if which == 0 else mx
        j = turn(own, k)
        node = along_y(j) if which == 0 else along_x(j)
        if which == 0:
            src, dst, into = grads.at[:, j, 2], ha.at[:, 1, my], ha.at[:, 1, j]
        else:
            src, dst, into = grads.at[j, :, 3], hb.at[:, 0, mx], hb.at[:, 0, j]
        if k == 0:
            move = pltpu.make_async_copy(src, dst, l_recv.at[which, own])
            if action == "start":
                move.start()
            elif action == "recv":
                move.wait()
        elif action == "start":
            copy_to(src, dst, l_send.at[which, j], l_recv.at[which, own], node).start()
        elif action == "recv":
            copy_to(into, into, l_send.at[which, j], l_recv.at[which, j], node).wait_recv()
        else:
            copy_to(src, src, l_send.at[which, j], l_recv.at[which, own], node).wait_send()

    def lines(kind, stage, action):
        own = my if kind < 2 else mx
        to = along_y if kind < 2 else along_x
        after, far, before = turn(own, 1), turn(own, 2), turn(own, 3)
        for way in range(2):
            if stage == 0:
                src, dst = part.at[kind, far, pl.ds(32 * way, 32)], mid.at[kind, way]
            else:
                src, dst = part.at[kind, before if way else after], sums.at[kind, way]
            number = 2 * stage + way
            move = copy_to(
                src, dst, p_send.at[kind, number], p_recv.at[kind, number], to(before if way else after)
            )
            if action == "start":
                move.start()
            elif action == "recv":
                move.wait_recv()
            else:
                move.wait_send()

    def pass_on(kind):
        lines(kind, 0, "recv")
        own = my if kind < 2 else mx
        for way in range(2):
            rows = pl.ds(32 * way, 32)
            there = turn(own, 3 if way else 1)
            part[kind, there, rows] = (part[kind, there, rows].astype(F32) + mid[kind, way].astype(F32)).astype(BF16)
        lines(kind, 1, "start")

    def onward(kind, k, action):
        own, to = (mx, along_x) if kind < 2 else (my, along_y)
        j = turn(own, k)

        def ends(sent, head):
            if kind < 2:
                return ha.at[sent, kind], back.at[kind, head]
            return hb.at[sent, 0], back.at[kind, :, head]

        src, dst = ends(j, own)
        if k == 0:
            move = pltpu.make_async_copy(src, dst, h_recv.at[kind, own])
            if action == "start":
                move.start()
            elif action == "recv":
                move.wait()
        elif action == "start":
            copy_to(src, dst, h_send.at[kind, j], h_recv.at[kind, own], to(j)).start()
        elif action == "recv":
            into = ends(j, j)[1]
            copy_to(into, into, h_send.at[kind, j], h_recv.at[kind, j], to(j)).wait_recv()
        else:
            copy_to(src, src, h_send.at[kind, j], h_recv.at[kind, own], to(j)).wait_send()

    for which in range(2):
        for k in (2, 1, 3, 0):
            late(which, k, "start")

    left_all = left[...]
    eig_terms = (lam * (left_all + acc_k[64:128])).astype(BF16)
    for t in range(NODES):
        tx, ty = divmod(t, SIDE)
        grads[tx, ty, 0] = eig_terms[:, t * TOK : (t + 1) * TOK]

    def multiply(kind):
        buf, index, rows_in = ((ha, 0, xlx), (ha, 1, xlx), (hb, 0, xly), (hb, 1, cly))[kind]
        lhs = jnp.concatenate([buf[g, index].reshape(SIDE * HS, TOK) for g in range(SIDE)], axis=1)
        product = dot(lhs, rows_in[...].reshape(SIDE * TOK, D))
        part[kind] = product.astype(BF16).reshape(SIDE, HS, D)
        lines(kind, 0, "start")

    for which in range(3):
        if which == 2:
            ring(2, 1, "recv")
        else:
            ring(which, 1, "recv")
    for k in range(SIDE):
        early_query(0, k, "recv")
        early_query(1, k, "recv")
        early_output_wait(k, "recv")
    multiply(0)
    multiply(3)
    for k in (2, 1, 3, 0):
        onward(0, k, "start")
    for which in range(2):
        for k in range(SIDE):
            late(which, k, "recv")
    pass_on(0)
    multiply(1)
    pass_on(3)
    multiply(2)
    for kind in (1, 2):
        for k in (2, 1, 3, 0):
            onward(kind, k, "start")
        pass_on(kind)

    def backward(t):
        return copy_to(grads.at[lax.div(t, SIDE), lax.rem(t, SIDE), 0], eigs.at[n], b_send.at[t], b_recv.at[n], t)

    def backward_self():
        return pltpu.make_async_copy(grads.at[mx, my, 0], eigs.at[n], b_recv.at[n])

    backward_self().start()

    @pl.loop(1, NODES)
    def _(k):
        backward(lax.rem(n + k, NODES)).start()

    weight_col = jnp.sum(eig_ref[...].astype(F32) * left_all, axis=1, keepdims=True)
    row_w = lax.broadcasted_iota(jnp.int32, (EIG, 128), 0)
    col_w = lax.broadcasted_iota(jnp.int32, (EIG, 128), 1)
    weight_row = jnp.sum(jnp.where(row_w == col_w, weight_col, 0.0), axis=0, keepdims=True)
    weight_high = weight_row.astype(BF16).astype(F32)
    row_g = lax.broadcasted_iota(jnp.int32, (16, 128), 0)
    weight_part = jnp.where(
        row_g == 0, weight_high, jnp.where(row_g == 1, weight_row - weight_high, 0.0)
    ).astype(BF16)

    def rows_of(group):
        return pl.ds(0, chunk + 16 * group)

    def swap(group):
        return pltpu.make_async_remote_copy(
            src_ref=gs.at[group, :, 1 - core, rows_of(group)], dst_ref=gx.at[group, :, rows_of(group)],
            send_sem=x_send.at[group], recv_sem=x_recv.at[group],
            device_id={"clus": chip * cores + 1 - core}, device_id_type=MESH,
        )

    def across(group, t):
        return pltpu.make_async_remote_copy(
            src_ref=gs.at[group, t, core, rows_of(group)], dst_ref=gr.at[group, chip, rows_of(group)],
            send_sem=c_send.at[group, t], recv_sem=c_recv.at[group, chip],
            device_id={"clus": t * cores + core}, device_id_type=MESH,
        )

    def across_in(group, s):
        return pltpu.make_async_remote_copy(
            src_ref=gr.at[group, s, rows_of(group)], dst_ref=gr.at[group, s, rows_of(group)],
            send_sem=c_send.at[group, s], recv_sem=c_recv.at[group, s],
            device_id={"clus": s * cores + core}, device_id_type=MESH,
        )

    def across_self(group):
        return pltpu.make_async_copy(
            gs.at[group, chip, core, rows_of(group)], gr.at[group, chip, rows_of(group)], c_recv.at[group, chip]
        )

    def across_start(group):
        if cores > 1:
            swap(group).wait_recv()
            for t in range(chips):
                both = gs[group, t, core, 0:chunk].astype(F32) + gx[group, t, 0:chunk].astype(F32)
                gs[group, t, core, 0:chunk] = both.astype(BF16)
            if group == 1:
                pair = gs[1, 0, core, chunk : chunk + 16].astype(F32) + gx[1, 0, chunk : chunk + 16].astype(F32)
                weight_sum = jnp.sum(pair, axis=0, keepdims=True)
                weight_top = weight_sum.astype(BF16).astype(F32)
                weight_both = jnp.where(
                    row_g == 0, weight_top, jnp.where(row_g == 1, weight_sum - weight_top, 0.0)
                ).astype(BF16)
                for t in range(chips):
                    gs[1, t, core, chunk : chunk + 16] = weight_both
        across_self(group).start()
        if chips > 1:
            @pl.loop(1, chips)
            def _(k):
                across(group, lax.rem(chip + k, chips)).start()

    for group, kinds in enumerate(((0, 3), (1, 2))):
        for kind in kinds:
            lines(kind, 1, "recv")
        for m in range(4):
            cols = slice(m * 256, (m + 1) * 256)
            stacked = []
            for kind in kinds:
                total = part[kind, my if kind < 2 else mx, :, cols].astype(F32)
                stacked.append(total + sums[kind, 0, :, cols].astype(F32) + sums[kind, 1, :, cols].astype(F32))
            g = jnp.concatenate(stacked, axis=0).T.astype(BF16)
            size = min(chunk, 256)
            for piece in range(256 // size):
                owner, lo = divmod(m * 256 + piece * size, chunk)
                gs[group, owner // cores, owner % cores, lo : lo + size, :] = g[piece * size : (piece + 1) * size]
                if lo + size == chunk and group == 1:
                    gs[group, owner // cores, owner % cores, chunk : chunk + 16, :] = weight_part
        if cores > 1:
            swap(group).start()
    across_start(0)
    across_start(1)

    for kind in range(3):
        for k in range(SIDE):
            onward(kind, k, "recv")
    for m in range(4):
        rows = slice(m * 256, (m + 1) * 256)
        total = dot(w[0, rows, :], back[0].reshape(D, TOK))
        total += dot(w[1, rows, :], back[1].reshape(D, TOK))
        total += dot(w[2, rows, :], back[2].reshape(D, TOK))
        gn_ref[:, rows] = total.T.astype(BF16)

    backward_self().wait()

    @pl.loop(1, NODES)
    def _(k):
        s = lax.rem(n + k, NODES)
        copy_to(eigs.at[s], eigs.at[s], b_send.at[s], b_recv.at[s], s).wait_recv()

    eig_total = eigs[0].astype(F32)
    for s in range(1, NODES):
        eig_total += eigs[s].astype(F32)
    ge_ref[...] = eig_total

    for group, kinds in enumerate(((0, 3), (1, 2))):
        across_self(group).wait()
        if chips > 1:
            @pl.loop(1, chips)
            def _(k):
                across_in(group, lax.rem(chip + k, chips)).wait_recv()

        used = slice(0, chunk + 16 * group)
        total = gr[group, 0, used].astype(F32)
        for s in range(1, chips):
            total += gr[group, s, used].astype(F32)
        gp_ref[kinds[0]] = total[0:chunk, 0:64]
        gp_ref[kinds[1]] = pltpu.roll(total[0:chunk], 64, 1)[:, 0:64]
        if group == 1:
            gw_ref[...] = (total[chunk : chunk + 1] + total[chunk + 1 : chunk + 2])[:, 0:64]

    for which in range(3):
        for stage in range(2):
            ring(which, stage, "send")
    for which in range(2):
        for k in range(1, SIDE):
            early_query(which, k, "sent")
            if which == 0:
                early_output_wait(k, "sent")
            late(which, k, "sent")
    for kind in range(4):
        for stage in range(2):
            lines(kind, stage, "sent")
    for kind in range(3):
        for k in range(1, SIDE):
            onward(kind, k, "sent")

    @pl.loop(1, NODES)
    def _(k):
        t = lax.rem(n + k, NODES)
        forward(t).wait_send()
        backward(t).wait_send()

    if cores > 1:
        swap(0).wait_send()
        swap(1).wait_send()
    if chips > 1:
        @pl.loop(1, chips)
        def _(k):
            across(0, lax.rem(chip + k, chips)).wait_send()
            across(1, lax.rem(chip + k, chips)).wait_send()


def outputs(*refs):
    for i in range(4):
        refs[4 + i][...] = refs[i][...]


def body(clusters, node_feats, cotangent, w_query, w_key, w_value, w_out, eigvec, eig_weight, block_mask):
    chunk = D // clusters
    cores = 2 if clusters % 2 == 0 else 1
    chips = clusters // cores
    anywhere = pl.BlockSpec(memory_space=pl.ANY)
    vmem = pl.BlockSpec(memory_space=pltpu.VMEM)
    dma = pltpu.SemaphoreType.DMA
    shapes = (
        jax.ShapeDtypeStruct((TOK, D), BF16),
        jax.ShapeDtypeStruct((EIG, TOK), F32),
        jax.ShapeDtypeStruct((1, EIG), F32),
        jax.ShapeDtypeStruct((4, chunk, HS), F32),
    )
    results = pl.pallas_call(
        functools.partial(kernel, clusters),
        out_shape=shapes,
        in_specs=[anywhere] * 6 + [vmem] * 3,
        out_specs=(vmem,) * 4,
        scratch_shapes=[
            pltpu.VMEM((4, D, D), BF16),
            pltpu.VMEM((SIDE, TOK, D), BF16),
            pltpu.VMEM((SIDE, TOK, D), BF16),
            pltpu.VMEM((SIDE, TOK, D), BF16),
            pltpu.VMEM((NODES, TOK, 256), BF16),
            pltpu.VMEM((NODES, TOK, 256), BF16),
            pltpu.VMEM((NC, 128), BF16),
            pltpu.VMEM((NC, 128), BF16),
            pltpu.VMEM((NC, 128), BF16),
            pltpu.VMEM((NC, 128), BF16),
            pltpu.VMEM((NC, 128), BF16),
            pltpu.VMEM((128, NC), BF16),
            pltpu.VMEM((64, NC), BF16),
            pltpu.VMEM((256, NC), BF16),
            pltpu.VMEM((128, NC), BF16),
            pltpu.VMEM((128, NC), F32),
            pltpu.VMEM((64, NC), F32),
            pltpu.VMEM((SIDE, SIDE, 5, HS, TOK), BF16),
            pltpu.VMEM((64, NC), F32),
            pltpu.VMEM((NODES, EIG, TOK), BF16),
            pltpu.VMEM((3, SIDE, SIDE, HS, TOK), BF16),
            pltpu.VMEM((SIDE, 2, SIDE, HS, TOK), BF16),
            pltpu.VMEM((SIDE, 2, SIDE, HS, TOK), BF16),
            pltpu.VMEM((4, SIDE, HS, D), BF16),
            pltpu.VMEM((4, 2, HS // 2, D), BF16),
            pltpu.VMEM((4, 2, HS, D), BF16),
            pltpu.VMEM((2, chips, cores, chunk + 16, 128), BF16),
            pltpu.VMEM((2, chips, chunk + 16, 128), BF16),
            pltpu.VMEM((2, chips, chunk + 16, 128), BF16),
            dma((3,)),
            dma((4, 4)),
            dma((3, 4)),
            dma((3, 4)),
            dma((NODES,)),
            dma((NODES,)),
            dma((NODES,)),
            dma((NODES,)),
            dma((SIDE,)),
            dma((SIDE,)),
            dma((2, SIDE)),
            dma((2, SIDE)),
            dma((2, SIDE)),
            dma((2, SIDE)),
            dma((4, SIDE)),
            dma((4, SIDE)),
            dma((3, SIDE)),
            dma((3, SIDE)),
            dma((2,)),
            dma((2,)),
            dma((2, chips)),
            dma((2, chips)),
        ],
        compiler_params=pltpu.CompilerParams(
            collective_id=0, has_side_effects=True, vmem_limit_bytes=60 * 1024 * 1024
        ),
        cost_estimate=pl.CostEstimate(flops=8 * 10**9, bytes_accessed=10**7, transcendentals=4 * 10**6),
    )(
        node_feats[0], cotangent[0], w_query, w_key, w_value, w_out,
        eigvec[0], eig_weight, block_mask[0, 0],
    )
    gn, ge, gw, gp = pl.pallas_call(
        outputs,
        out_shape=shapes,
        in_specs=[vmem] * 4,
        out_specs=(vmem,) * 4,
    )(*results)
    return gn[None], ge[None], gw, gp


def solution(mesh):
    placed = (
        P("clus", "node", None),
        P("clus", "node", None),
        P(),
        P(),
        P(),
        P(),
        P("clus", None, None),
        P("node", None),
        P("clus", "node", None, None),
    )
    return jax.shard_map(
        functools.partial(body, mesh.shape["clus"]),
        mesh=mesh,
        in_specs=placed,
        out_specs=(
            P("clus", "node", None),
            P("clus", None, "node"),
            P("node", None),
            P(None, "clus", "node"),
        ),
        check_vma=False,
    )
```

```python
import functools

import jax
import jax.numpy as jnp
from jax import lax
from jax.experimental import pallas as pl
from jax.experimental.pallas import tpu as pltpu
from jax.sharding import PartitionSpec as P

MESH = pl.DeviceIdType.MESH
F32 = jnp.float32
BF16 = jnp.bfloat16
ABSENT = -(2.0**100)
SIDE = 4
NODES = 16
TOK = 128
D = 1024
NC = 2048
EIG = 64
HS = 64
SCALE = HS**-0.5
ROWS = 512
ORDER = (2, 1, 3, 0)


def dot(a, b):
    return lax.dot_general(a, b, (((1,), (0,)), ((), ())), preferred_element_type=F32)


def kernel(
    clusters,
    x_hbm, cot_hbm, wq_hbm, wk_hbm, wv_hbm, wo_hbm, eig_ref, lam_ref, mask_ref,
    gn_ref, ge_ref, gw_ref, gp_ref,
    w, xlx, xly, cly, send, recv, eigt, qe, d0, ke, bm, eqt, dt, kt, bt,
    acc_k, acc_v, grads, left, eigs, back, ha, hb, part, mid, sums, gs, gx, gr,
    in_sem, w_sem, ring_send, ring_recv, f_send, f_recv, b_send, b_recv, o_send, o_recv, q_send, q_recv, l_send, l_recv,
    p_send, p_recv, h_send, h_recv, x_send, x_recv, c_send, c_recv,
):
    n = lax.axis_index("node")
    c = lax.axis_index("clus")
    mx = lax.div(n, SIDE)
    my = lax.rem(n, SIDE)
    chunk = D // clusters
    cores = 2 if clusters % 2 == 0 else 1
    chips = clusters // cores
    chip, core = lax.div(c, cores), lax.rem(c, cores)

    def turn(i, by):
        return lax.rem(i + by, SIDE)

    loads = [
        pltpu.make_async_copy(x_hbm, xlx.at[mx], in_sem.at[0]),
        pltpu.make_async_copy(x_hbm, xly.at[my], in_sem.at[1]),
        pltpu.make_async_copy(cot_hbm, cly.at[my], in_sem.at[2]),
    ]
    for load in loads:
        load.start()
    w_hbm = (wq_hbm, wk_hbm, wv_hbm, wo_hbm)

    def w_copy(t, k):
        cols = pl.ds(pl.multiple_of(turn(mx, k) * 256, 256), 256)
        return pltpu.make_async_copy(w_hbm[t].at[:, cols], w.at[t, :, cols], w_sem.at[t, k])

    for t in range(4):
        w_copy(t, ORDER[0]).start()

    barrier = pltpu.get_barrier_semaphore()

    @pl.loop(1, NODES)
    def _(k):
        pl.semaphore_signal(barrier, inc=1, device_id={"node": lax.rem(n + k, NODES)}, device_id_type=MESH)

    if clusters > 1:
        @pl.loop(1, clusters)
        def _(k):
            pl.semaphore_signal(
                barrier, inc=1, device_id={"clus": lax.rem(c + k, clusters)}, device_id_type=MESH
            )

    row_id = lax.broadcasted_iota(jnp.int32, (EIG, EIG), 0)
    col_id = lax.broadcasted_iota(jnp.int32, (EIG, EIG), 1)
    lam = jnp.sum(jnp.where(row_id == col_id, lam_ref[...], 0.0), axis=1, keepdims=True)
    kt[64:128, :] = (lam * eig_ref[...].astype(F32)).astype(BF16)
    kt[144:256, :] = jnp.zeros((112, NC), BF16)
    bias = jnp.where(mask_ref[...] > 0, 0.0, ABSENT)
    for j in range(NODES):
        kt[128:144, j * TOK : (j + 1) * TOK] = jnp.broadcast_to(bias[:, j : j + 1], (16, TOK)).astype(BF16)
        eig_part = eig_ref[:, j * TOK : (j + 1) * TOK].astype(F32)
        full = jnp.concatenate([jnp.zeros((64, TOK), F32), eig_part], axis=0)
        eigt[j * TOK : (j + 1) * TOK, :] = full.T.astype(BF16)
    eqt[64:128, :] = eig_ref[...]

    for load in loads:
        load.wait()
    pl.semaphore_wait(barrier, NODES - 1 + clusters - 1)

    def copy_to(src, dst, send_sem, recv_sem, node):
        return pltpu.make_async_remote_copy(
            src_ref=src, dst_ref=dst, send_sem=send_sem, recv_sem=recv_sem,
            device_id={"node": node}, device_id_type=MESH,
        )

    def along_x(x):
        return x * SIDE + my

    def along_y(y):
        return mx * SIDE + y

    rings = []
    for buf, at, to in ((xlx, mx, along_x), (xly, my, along_y), (cly, my, along_y)):
        before, after, far = turn(at, 3), turn(at, 1), turn(at, 2)
        rings.append((
            ((0, buf.at[at], buf.at[before], to(after)), (1, buf.at[at], buf.at[after], to(before))),
            ((2, buf.at[before, pl.ds(0, 64)], buf.at[far, pl.ds(0, 64)], to(after)),
             (3, buf.at[after, pl.ds(64, 64)], buf.at[far, pl.ds(64, 64)], to(before))),
        ))

    def ring(which, stage, action):
        for number, out, into, node in rings[which][stage]:
            sems = ring_send.at[which, number], ring_recv.at[which, number]
            if action == "start":
                copy_to(out, out, *sems, node).start()
            elif action == "recv":
                copy_to(into, into, *sems, node).wait_recv()
            else:
                copy_to(out, out, *sems, node).wait_send()

    ring(0, 0, "start")
    ring(1, 0, "start")

    low = lax.broadcasted_iota(jnp.int32, (TOK, 128), 1) < 64

    def forward(t):
        return copy_to(send.at[t], recv.at[n], f_send.at[t], f_recv.at[n], t)

    def forward_self():
        return pltpu.make_async_copy(send.at[n], recv.at[n], f_recv.at[n])

    for at, k in enumerate(ORDER):
        first = turn(mx, k) * SIDE
        cols = pl.ds(pl.multiple_of(first * HS, 256), 256)
        rows_x = xly[my]
        parts = []
        for t in range(4):
            w_copy(t, k).wait()
            if at + 1 < SIDE:
                w_copy(t, ORDER[at + 1]).start()
            product = dot(rows_x if t < 3 else cly[my], w[t, :, cols])
            parts.append(product * SCALE if t == 0 else product)
        for pair in range(2):
            q, kk, v, d = (a[:, pair * 128 : (pair + 1) * 128] for a in parts)
            qs, ks, vs, ds = (pltpu.roll(a, 64, 1) for a in (q, kk, v, d))
            t0 = first + 2 * pair
            send[t0, :, 0:128] = jnp.where(low, q, ds).astype(BF16)
            send[t0, :, 128:256] = jnp.where(low, kk, vs).astype(BF16)
            send[t0 + 1, :, 0:128] = jnp.where(low, qs, d).astype(BF16)
            send[t0 + 1, :, 128:256] = jnp.where(low, ks, v).astype(BF16)
        for j in range(SIDE):
            t = first + j

            @pl.when(t != n)
            def _():
                forward(t).start()

            @pl.when(t == n)
            def _():
                forward_self().start()

    acc_k[...] = jnp.zeros_like(acc_k)
    acc_v[...] = jnp.zeros_like(acc_v)

    @pl.loop(0, NODES)
    def _(k):
        s = lax.rem(n + k, NODES)

        @pl.when(s != n)
        def _():
            copy_to(recv.at[s], recv.at[s], f_send.at[s], f_recv.at[s], s).wait_recv()

        @pl.when(s == n)
        def _():
            forward_self().wait()

        rows = pl.ds(pl.multiple_of(s * TOK, TOK), TOK)
        a = recv[s, :, 0:128].astype(F32)
        b = recv[s, :, 128:256].astype(F32)
        e = eigt[rows, :].astype(F32)
        qe[rows, :] = jnp.where(low, a, e).astype(BF16)
        ke[rows, :] = jnp.where(low, b, e).astype(BF16)
        d0[rows, :] = jnp.where(low, 0.0, a).astype(BF16)
        bm[rows, :] = b.astype(BF16)
        at = a.T.astype(BF16)
        b_t = b.T.astype(BF16)
        eqt[0:64, rows] = at[0:64]
        dt[:, rows] = at[64:128]
        kt[0:64, rows] = b_t[0:64]
        bt[:, rows] = b_t

    ring(0, 0, "recv")
    ring(1, 0, "recv")
    ring(2, 0, "start")
    ring(0, 1, "start")
    ring(1, 1, "start")

    def early_output(tx):
        src, dst = grads.at[tx, :, 4], hb.at[:, 1, mx]

        @pl.when(tx != mx)
        def _():
            copy_to(src, dst, o_send.at[tx], o_recv.at[mx], along_x(tx)).start()

        @pl.when(tx == mx)
        def _():
            pltpu.make_async_copy(src, dst, o_recv.at[mx]).start()

    def early_output_wait(k, action):
        j = turn(mx, k)
        into = hb.at[:, 1, j]
        if k == 0:
            if action == "recv":
                pltpu.make_async_copy(grads.at[mx, :, 4], into, o_recv.at[mx]).wait()
        elif action == "recv":
            copy_to(into, into, o_send.at[j], o_recv.at[j], along_x(j)).wait_recv()
        else:
            src = grads.at[j, :, 4]
            copy_to(src, src, o_send.at[j], o_recv.at[mx], along_x(j)).wait_send()

    def early_query(half, k, action):
        j = turn(my, k)
        groups = pl.ds(2 * half, 2)
        src, dst, into = grads.at[groups, j, 1], ha.at[groups, 0, my], ha.at[groups, 0, j]
        if k == 0:
            move = pltpu.make_async_copy(src, dst, q_recv.at[half, my])
            if action == "start":
                move.start()
            elif action == "recv":
                move.wait()
        elif action == "start":
            copy_to(src, dst, q_send.at[half, j], q_recv.at[half, my], along_y(j)).start()
        elif action == "recv":
            copy_to(into, into, q_send.at[half, j], q_recv.at[half, j], along_y(j)).wait_recv()
        else:
            copy_to(src, src, q_send.at[half, j], q_recv.at[half, my], along_y(j)).wait_send()

    lane = lax.broadcasted_iota(jnp.int32, (ROWS, 128), 1)
    sub = lax.div(lax.broadcasted_iota(jnp.int32, (ROWS, 128), 0), TOK)
    steps = NC // ROWS

    @pl.loop(0, steps)
    def _(i):
        @pl.when(i == steps - 1)
        def _():
            ring(2, 0, "recv")
            ring(2, 1, "start")

        rows = pl.ds(pl.multiple_of(i * ROWS, ROWS), ROWS)
        tile = jnp.where(lane == sub + i * (ROWS // TOK), 1.0, 0.0).astype(BF16)
        scores = dot(jnp.concatenate([qe[rows, :], tile], axis=1), kt[...])
        dprob = dot(d0[rows, :], bt[...])
        raised = jnp.exp(scores - jnp.max(scores, axis=1, keepdims=True))
        inverse = 1.0 / jnp.sum(raised, axis=1, keepdims=True)
        prob = raised * inverse
        delta = jnp.sum(prob * dprob, axis=1, keepdims=True)
        half = prob.astype(BF16)
        dscore = (prob * (dprob - delta)).astype(BF16)
        out = dot(half, bm[...])
        grad_q = dot(dscore, ke[...])
        acc_k[...] += dot(eqt[:, rows], dscore)
        acc_v[...] += dot(dt[:, rows], half)
        grad_qt = grad_q.T
        left[:, rows] = grad_qt[64:128]
        out_t = out.T
        for j in range(ROWS // TOK):
            t = i * (ROWS // TOK) + j
            cols = slice(j * TOK, (j + 1) * TOK)
            tx, ty = lax.div(t, SIDE), lax.rem(t, SIDE)
            grads[tx, ty, 1] = (grad_qt[0:64, cols] * SCALE).astype(BF16)
            grads[tx, ty, 4] = out_t[64:128, cols].astype(BF16)

        early_output(i)

        @pl.when(i == steps // 2 - 1)
        def _():
            for k in (2, 1, 3, 0):
                early_query(0, k, "start")

    for k in (2, 1, 3, 0):
        early_query(1, k, "start")
    for t in range(NODES):
        cols = slice(t * TOK, (t + 1) * TOK)
        tx, ty = divmod(t, SIDE)
        grads[tx, ty, 2] = acc_k[0:64, cols].astype(BF16)
        grads[tx, ty, 3] = acc_v[:, cols].astype(BF16)

    def late(which, k, action):
        own = my if which == 0 else mx
        j = turn(own, k)
        node = along_y(j) if which == 0 else along_x(j)
        if which == 0:
            src, dst, into = grads.at[:, j, 2], ha.at[:, 1, my], ha.at[:, 1, j]
        else:
            src, dst, into = grads.at[j, :, 3], hb.at[:, 0, mx], hb.at[:, 0, j]
        if k == 0:
            move = pltpu.make_async_copy(src, dst, l_recv.at[which, own])
            if action == "start":
                move.start()
            elif action == "recv":
                move.wait()
        elif action == "start":
            copy_to(src, dst, l_send.at[which, j], l_recv.at[which, own], node).start()
        elif action == "recv":
            copy_to(into, into, l_send.at[which, j], l_recv.at[which, j], node).wait_recv()
        else:
            copy_to(src, src, l_send.at[which, j], l_recv.at[which, own], node).wait_send()

    def lines(kind, stage, action):
        own = my if kind < 2 else mx
        to = along_y if kind < 2 else along_x
        after, far, before = turn(own, 1), turn(own, 2), turn(own, 3)
        for way in range(2):
            if stage == 0:
                src, dst = part.at[kind, far, pl.ds(32 * way, 32)], mid.at[kind, way]
            else:
                src, dst = part.at[kind, before if way else after], sums.at[kind, way]
            number = 2 * stage + way
            move = copy_to(
                src, dst, p_send.at[kind, number], p_recv.at[kind, number], to(before if way else after)
            )
            if action == "start":
                move.start()
            elif action == "recv":
                move.wait_recv()
            else:
                move.wait_send()

    def pass_on(kind):
        lines(kind, 0, "recv")
        own = my if kind < 2 else mx
        for way in range(2):
            rows = pl.ds(32 * way, 32)
            there = turn(own, 3 if way else 1)
            part[kind, there, rows] = (part[kind, there, rows].astype(F32) + mid[kind, way].astype(F32)).astype(BF16)
        lines(kind, 1, "start")

    def onward(kind, k, action):
        own, to = (mx, along_x) if kind < 2 else (my, along_y)
        j = turn(own, k)

        def ends(sent, head):
            if kind < 2:
                return ha.at[sent, kind], back.at[kind, head]
            return hb.at[sent, 0], back.at[kind, :, head]

        src, dst = ends(j, own)
        if k == 0:
            move = pltpu.make_async_copy(src, dst, h_recv.at[kind, own])
            if action == "start":
                move.start()
            elif action == "recv":
                move.wait()
        elif action == "start":
            copy_to(src, dst, h_send.at[kind, j], h_recv.at[kind, own], to(j)).start()
        elif action == "recv":
            into = ends(j, j)[1]
            copy_to(into, into, h_send.at[kind, j], h_recv.at[kind, j], to(j)).wait_recv()
        else:
            copy_to(src, src, h_send.at[kind, j], h_recv.at[kind, own], to(j)).wait_send()

    for which in range(2):
        for k in (2, 1, 3, 0):
            late(which, k, "start")

    left_all = left[...]
    eig_terms = (lam * (left_all + acc_k[64:128])).astype(BF16)
    for t in range(NODES):
        tx, ty = divmod(t, SIDE)
        grads[tx, ty, 0] = eig_terms[:, t * TOK : (t + 1) * TOK]

    def multiply(kind):
        buf, index, rows_in = ((ha, 0, xlx), (ha, 1, xlx), (hb, 0, xly), (hb, 1, cly))[kind]
        lhs = jnp.concatenate([buf[g, index].reshape(SIDE * HS, TOK) for g in range(SIDE)], axis=1)
        product = dot(lhs, rows_in[...].reshape(SIDE * TOK, D))
        part[kind] = product.astype(BF16).reshape(SIDE, HS, D)
        lines(kind, 0, "start")

    for which in range(3):
        if which == 2:
            ring(2, 1, "recv")
        else:
            ring(which, 1, "recv")
    for k in range(SIDE):
        early_query(0, k, "recv")
        early_query(1, k, "recv")
        early_output_wait(k, "recv")
    multiply(0)
    multiply(3)
    for k in (2, 1, 3, 0):
        onward(0, k, "start")
    for which in range(2):
        for k in range(SIDE):
            late(which, k, "recv")
    pass_on(0)
    multiply(1)
    pass_on(3)
    multiply(2)
    for kind in (1, 2):
        for k in (2, 1, 3, 0):
            onward(kind, k, "start")
        pass_on(kind)

    def backward(t):
        return copy_to(grads.at[lax.div(t, SIDE), lax.rem(t, SIDE), 0], eigs.at[n], b_send.at[t], b_recv.at[n], t)

    def backward_self():
        return pltpu.make_async_copy(grads.at[mx, my, 0], eigs.at[n], b_recv.at[n])

    backward_self().start()

    @pl.loop(1, NODES)
    def _(k):
        backward(lax.rem(n + k, NODES)).start()

    weight_col = jnp.sum(eig_ref[...].astype(F32) * left_all, axis=1, keepdims=True)
    row_w = lax.broadcasted_iota(jnp.int32, (EIG, 128), 0)
    col_w = lax.broadcasted_iota(jnp.int32, (EIG, 128), 1)
    weight_row = jnp.sum(jnp.where(row_w == col_w, weight_col, 0.0), axis=0, keepdims=True)
    weight_high = weight_row.astype(BF16).astype(F32)
    row_g = lax.broadcasted_iota(jnp.int32, (16, 128), 0)
    weight_part = jnp.where(
        row_g == 0, weight_high, jnp.where(row_g == 1, weight_row - weight_high, 0.0)
    ).astype(BF16)

    def rows_of(group):
        return pl.ds(0, chunk + 16 * group)

    def swap(group):
        return pltpu.make_async_remote_copy(
            src_ref=gs.at[group, :, 1 - core, rows_of(group)], dst_ref=gx.at[group, :, rows_of(group)],
            send_sem=x_send.at[group], recv_sem=x_recv.at[group],
            device_id={"clus": chip * cores + 1 - core}, device_id_type=MESH,
        )

    def across(group, t):
        return pltpu.make_async_remote_copy(
            src_ref=gs.at[group, t, core, rows_of(group)], dst_ref=gr.at[group, chip, rows_of(group)],
            send_sem=c_send.at[group, t], recv_sem=c_recv.at[group, chip],
            device_id={"clus": t * cores + core}, device_id_type=MESH,
        )

    def across_in(group, s):
        return pltpu.make_async_remote_copy(
            src_ref=gr.at[group, s, rows_of(group)], dst_ref=gr.at[group, s, rows_of(group)],
            send_sem=c_send.at[group, s], recv_sem=c_recv.at[group, s],
            device_id={"clus": s * cores + core}, device_id_type=MESH,
        )

    def across_self(group):
        return pltpu.make_async_copy(
            gs.at[group, chip, core, rows_of(group)], gr.at[group, chip, rows_of(group)], c_recv.at[group, chip]
        )

    def across_start(group):
        if cores > 1:
            swap(group).wait_recv()
            for t in range(chips):
                both = gs[group, t, core, 0:chunk].astype(F32) + gx[group, t, 0:chunk].astype(F32)
                gs[group, t, core, 0:chunk] = both.astype(BF16)
            if group == 1:
                pair = gs[1, 0, core, chunk : chunk + 16].astype(F32) + gx[1, 0, chunk : chunk + 16].astype(F32)
                weight_sum = jnp.sum(pair, axis=0, keepdims=True)
                weight_top = weight_sum.astype(BF16).astype(F32)
                weight_both = jnp.where(
                    row_g == 0, weight_top, jnp.where(row_g == 1, weight_sum - weight_top, 0.0)
                ).astype(BF16)
                for t in range(chips):
                    gs[1, t, core, chunk : chunk + 16] = weight_both
        across_self(group).start()
        if chips > 1:
            @pl.loop(1, chips)
            def _(k):
                across(group, lax.rem(chip + k, chips)).start()

    for group, kinds in enumerate(((0, 3), (1, 2))):
        for kind in kinds:
            lines(kind, 1, "recv")
        for m in range(4):
            cols = slice(m * 256, (m + 1) * 256)
            stacked = []
            for kind in kinds:
                total = part[kind, my if kind < 2 else mx, :, cols].astype(F32)
                stacked.append(total + sums[kind, 0, :, cols].astype(F32) + sums[kind, 1, :, cols].astype(F32))
            g = jnp.concatenate(stacked, axis=0).T.astype(BF16)
            size = min(chunk, 256)
            for piece in range(256 // size):
                owner, lo = divmod(m * 256 + piece * size, chunk)
                gs[group, owner // cores, owner % cores, lo : lo + size, :] = g[piece * size : (piece + 1) * size]
                if lo + size == chunk and group == 1:
                    gs[group, owner // cores, owner % cores, chunk : chunk + 16, :] = weight_part
        if cores > 1:
            swap(group).start()
    across_start(0)
    across_start(1)

    for kind in range(3):
        for k in range(SIDE):
            onward(kind, k, "recv")
    for m in range(4):
        rows = slice(m * 256, (m + 1) * 256)
        total = dot(w[0, rows, :], back[0].reshape(D, TOK))
        total += dot(w[1, rows, :], back[1].reshape(D, TOK))
        total += dot(w[2, rows, :], back[2].reshape(D, TOK))
        gn_ref[:, rows] = total.T.astype(BF16)

    backward_self().wait()

    @pl.loop(1, NODES)
    def _(k):
        s = lax.rem(n + k, NODES)
        copy_to(eigs.at[s], eigs.at[s], b_send.at[s], b_recv.at[s], s).wait_recv()

    eig_total = eigs[0].astype(F32)
    for s in range(1, NODES):
        eig_total += eigs[s].astype(F32)
    ge_ref[...] = eig_total

    for group, kinds in enumerate(((0, 3), (1, 2))):
        across_self(group).wait()
        if chips > 1:
            @pl.loop(1, chips)
            def _(k):
                across_in(group, lax.rem(chip + k, chips)).wait_recv()

        used = slice(0, chunk + 16 * group)
        total = gr[group, 0, used].astype(F32)
        for s in range(1, chips):
            total += gr[group, s, used].astype(F32)
        gp_ref[kinds[0]] = total[0:chunk, 0:64]
        gp_ref[kinds[1]] = pltpu.roll(total[0:chunk], 64, 1)[:, 0:64]
        if group == 1:
            gw_ref[...] = (total[chunk : chunk + 1] + total[chunk + 1 : chunk + 2])[:, 0:64]

    for which in range(3):
        for stage in range(2):
            ring(which, stage, "send")
    for which in range(2):
        for k in range(1, SIDE):
            early_query(which, k, "sent")
            if which == 0:
                early_output_wait(k, "sent")
            late(which, k, "sent")
    for kind in range(4):
        for stage in range(2):
            lines(kind, stage, "sent")
    for kind in range(3):
        for k in range(1, SIDE):
            onward(kind, k, "sent")

    @pl.loop(1, NODES)
    def _(k):
        t = lax.rem(n + k, NODES)
        forward(t).wait_send()
        backward(t).wait_send()

    if cores > 1:
        swap(0).wait_send()
        swap(1).wait_send()
    if chips > 1:
        @pl.loop(1, chips)
        def _(k):
            across(0, lax.rem(chip + k, chips)).wait_send()
            across(1, lax.rem(chip + k, chips)).wait_send()


def outputs(*refs):
    for i in range(4):
        refs[4 + i][...] = refs[i][...]


def body(clusters, node_feats, cotangent, w_query, w_key, w_value, w_out, eigvec, eig_weight, block_mask):
    chunk = D // clusters
    cores = 2 if clusters % 2 == 0 else 1
    chips = clusters // cores
    anywhere = pl.BlockSpec(memory_space=pl.ANY)
    vmem = pl.BlockSpec(memory_space=pltpu.VMEM)
    dma = pltpu.SemaphoreType.DMA
    shapes = (
        jax.ShapeDtypeStruct((TOK, D), BF16),
        jax.ShapeDtypeStruct((EIG, TOK), F32),
        jax.ShapeDtypeStruct((1, EIG), F32),
        jax.ShapeDtypeStruct((4, chunk, HS), F32),
    )
    results = pl.pallas_call(
        functools.partial(kernel, clusters),
        out_shape=shapes,
        in_specs=[anywhere] * 6 + [vmem] * 3,
        out_specs=(vmem,) * 4,
        scratch_shapes=[
            pltpu.VMEM((4, D, D), BF16),
            pltpu.VMEM((SIDE, TOK, D), BF16),
            pltpu.VMEM((SIDE, TOK, D), BF16),
            pltpu.VMEM((SIDE, TOK, D), BF16),
            pltpu.VMEM((NODES, TOK, 256), BF16),
            pltpu.VMEM((NODES, TOK, 256), BF16),
            pltpu.VMEM((NC, 128), BF16),
            pltpu.VMEM((NC, 128), BF16),
            pltpu.VMEM((NC, 128), BF16),
            pltpu.VMEM((NC, 128), BF16),
            pltpu.VMEM((NC, 128), BF16),
            pltpu.VMEM((128, NC), BF16),
            pltpu.VMEM((64, NC), BF16),
            pltpu.VMEM((256, NC), BF16),
            pltpu.VMEM((128, NC), BF16),
            pltpu.VMEM((128, NC), F32),
            pltpu.VMEM((64, NC), F32),
            pltpu.VMEM((SIDE, SIDE, 5, HS, TOK), BF16),
            pltpu.VMEM((64, NC), F32),
            pltpu.VMEM((NODES, EIG, TOK), BF16),
            pltpu.VMEM((3, SIDE, SIDE, HS, TOK), BF16),
            pltpu.VMEM((SIDE, 2, SIDE, HS, TOK), BF16),
            pltpu.VMEM((SIDE, 2, SIDE, HS, TOK), BF16),
            pltpu.VMEM((4, SIDE, HS, D), BF16),
            pltpu.VMEM((4, 2, HS // 2, D), BF16),
            pltpu.VMEM((4, 2, HS, D), BF16),
            pltpu.VMEM((2, chips, cores, chunk + 16, 128), BF16),
            pltpu.VMEM((2, chips, chunk + 16, 128), BF16),
            pltpu.VMEM((2, chips, chunk + 16, 128), BF16),
            dma((3,)),
            dma((4, 4)),
            dma((3, 4)),
            dma((3, 4)),
            dma((NODES,)),
            dma((NODES,)),
            dma((NODES,)),
            dma((NODES,)),
            dma((SIDE,)),
            dma((SIDE,)),
            dma((2, SIDE)),
            dma((2, SIDE)),
            dma((2, SIDE)),
            dma((2, SIDE)),
            dma((4, SIDE)),
            dma((4, SIDE)),
            dma((3, SIDE)),
            dma((3, SIDE)),
            dma((2,)),
            dma((2,)),
            dma((2, chips)),
            dma((2, chips)),
        ],
        compiler_params=pltpu.CompilerParams(
            collective_id=0, has_side_effects=True, vmem_limit_bytes=60 * 1024 * 1024
        ),
        cost_estimate=pl.CostEstimate(flops=8 * 10**9, bytes_accessed=10**7, transcendentals=4 * 10**6),
    )(
        node_feats[0], cotangent[0], w_query, w_key, w_value, w_out,
        eigvec[0], eig_weight, block_mask[0, 0],
    )
    gn, ge, gw, gp = pl.pallas_call(
        outputs,
        out_shape=shapes,
        in_specs=[vmem] * 4,
        out_specs=(vmem,) * 4,
    )(*results)
    return gn[None], ge[None], gw, gp


def solution(mesh):
    placed = (
        P("clus", "node", None),
        P("clus", "node", None),
        P(),
        P(),
        P(),
        P(),
        P("clus", None, None),
        P("node", None),
        P("clus", "node", None, None),
    )
    return jax.shard_map(
        functools.partial(body, mesh.shape["clus"]),
        mesh=mesh,
        in_specs=placed,
        out_specs=(
            P("clus", "node", None),
            P("clus", None, "node"),
            P("node", None),
            P(None, "clus", "node"),
        ),
        check_vma=False,
    )
```
